32 devices in a mesh: groups: 2 (over x), tiles: 16 (over z, y, core).
Axes of the slice: x: 2, y: 2, z: 4, core: 2. Of those that a mesh axis runs over, the one named last changes fastest.
Arguments:
- water_state: float32 [64, 3, 256, 256], P('groups', None, 'tiles'), parts along dimension 0, may hold values from -3 to 3, as said below
- terrain: float32 [64, 2, 256, 256], P('groups', None, 'tiles'), parts along dimension 0, may hold values from -1 to 1, as said below
- work_list: int32 [32], P('groups'), parts along dimension 0, may hold values from 0 to 32, as said below
- edge_kind: int32 [64, 4], P('groups'), parts along dimension 0, may hold values from 0 to 2, as said below
Outputs:
- stepped_water: float32 [64, 3, 256, 256], P('groups', None, 'tiles'), parts along dimension 0
The draws below stay inside these ranges and needn't reach their ends.
There are 2 independent parts, one for each index of `groups`. The reference program is written for one: setup_inputs(seed, part) draws one part's arguments, and reference() takes and returns one part's arrays. A program takes and returns all parts, laid end to end along the dimension named above; each array names one. Nothing has to cross between parts.
Inputs may be any that keep to these rules, and one draw needn't show every extreme that they name: `work_list`: entry w + s is slot s of index w of tiles. No tile appears twice; the value 32 marks an empty slot and occurs only in a last slot; some index has all its slots filled. `edge_kind`: kind 1 (open) stands only between two listed tiles and is the same on both sides of their edge; a listed tile's edge on the window's boundary is 0 (wall) or 2 (outflow); an edge towards an unlisted tile is 0. `water_state`: component 0 is depth, 0.1 or more; components 1 and 2 are discharges. `terrain`: component 0 is bed elevation; component 1 is a Manning coefficient from 0.03 to 0.3.
All inputs are finite; a program needn't handle non-finite values.
Results may differ from the reference program's by a relative error of at most 0.00002.
Values sent between devices are 32-bit elements; how exact they have to be, the bound alone decides.
A program may use at most 64 MiB of HBM per device.

```python
import jax
import jax.numpy as jnp
from jax import lax

S = 256
TW = 16
ITERS = 4
NT = 32
TH = 2
SLOTS = 1
LISTED = 16
N_TILES = 16


def tile_layout(key):
    subkeys = jax.random.split(jax.random.fold_in(key, 17), 8)
    tile_ids = jnp.arange(NT, dtype=jnp.int32)
    tile_row = tile_ids // TW
    tile_col = tile_ids % TW
    centre_row = jax.random.randint(subkeys[0], (), 0, TH, dtype=jnp.int32)
    centre_col = jax.random.randint(subkeys[1], (), 0, TW, dtype=jnp.int32)
    shuffle = jax.random.permutation(subkeys[2], NT).astype(jnp.int32)
    scores = (jnp.abs(tile_row - centre_row) + jnp.abs(tile_col - centre_col)) * NT + shuffle
    tile_ranks = jnp.argsort(jnp.argsort(scores)).astype(jnp.int32)
    wet_count = LISTED - jax.random.randint(subkeys[3], (), 0, max(N_TILES // 2, 1), dtype=jnp.int32)
    is_wet = tile_ranks < wet_count
    ordered = jnp.sort(jnp.where(is_wet, tile_ids, NT + tile_ids))[:LISTED]
    serial = jnp.arange(LISTED, dtype=jnp.int32)
    owners = jax.random.permutation(subkeys[4], N_TILES).astype(jnp.int32)
    places = owners[serial % N_TILES] * SLOTS + serial // N_TILES
    entries = jnp.where(serial < wet_count, ordered, NT).astype(jnp.int32)
    work_slots = jnp.full((LISTED,), NT, jnp.int32).at[places].set(entries)
    wet_grid = is_wet.reshape(TH, TW)
    downward = jax.random.randint(subkeys[5], (TH, TW), 0, 4, dtype=jnp.int32) > 0
    sideways = jax.random.randint(subkeys[6], (TH, TW), 0, 4, dtype=jnp.int32) > 0
    border = jax.random.randint(subkeys[7], (TH, TW, 4), 0, 2, dtype=jnp.int32) * 2
    false_row = jnp.zeros((1, TW), dtype=bool)
    false_column = jnp.zeros((TH, 1), dtype=bool)
    north_open = jnp.concatenate([false_row, downward[:-1] & wet_grid[:-1]], axis=0) & wet_grid
    south_open = jnp.concatenate([downward[:-1] & wet_grid[1:], false_row], axis=0) & wet_grid
    west_open = jnp.concatenate([false_column, sideways[:, :-1] & wet_grid[:, :-1]], axis=1) & wet_grid
    east_open = jnp.concatenate([sideways[:, :-1] & wet_grid[:, 1:], false_column], axis=1) & wet_grid
    grid_rows = jnp.arange(TH, dtype=jnp.int32)[:, None]
    grid_columns = jnp.arange(TW, dtype=jnp.int32)[None, :]

    def edge_value(opened, at_edge, extra):
        inner = jnp.where(opened, 1, 0).astype(jnp.int32)
        outer = jnp.where(wet_grid, extra, 0).astype(jnp.int32)
        return jnp.where(at_edge, outer, inner)
    north_kind = edge_value(north_open, grid_rows == 0, border[..., 0])
    south_kind = edge_value(south_open, grid_rows == TH - 1, border[..., 1])
    west_kind = edge_value(west_open, grid_columns == 0, border[..., 2])
    east_kind = edge_value(east_open, grid_columns == TW - 1, border[..., 3])
    side_kinds = jnp.stack([north_kind, south_kind, west_kind, east_kind], axis=-1).reshape(NT, 4).astype(jnp.int32)
    return (work_slots, side_kinds)


def draw_work_list(key, part):
    return tile_layout(key)[0]


def draw_edge_kind(key, part):
    return tile_layout(key)[1]


def draw_water_state(key, part):
    subkeys = jax.random.split(jax.random.fold_in(key, 23), 4)
    tile_depth = jnp.exp(jax.random.uniform(subkeys[2], (NT, 1, 1, 1), jnp.float32, jnp.log(0.12), jnp.log(2.0)))
    tile_flow = jnp.exp(jax.random.uniform(subkeys[3], (NT, 1, 1, 1), jnp.float32, jnp.log(0.2), jnp.log(1.0)))
    water_depth = jnp.clip(tile_depth * jnp.exp(jax.random.uniform(subkeys[0], (NT, 1, S, S), jnp.float32, -0.5, 0.5)), 0.1, 3.0)
    discharge = tile_flow * jnp.clip(0.6 * jax.random.normal(subkeys[1], (NT, 2, S, S), jnp.float32), -2.5, 2.5)
    return jnp.concatenate([water_depth, discharge], axis=1).astype(jnp.float32)


def draw_terrain(key, part):
    subkeys = jax.random.split(jax.random.fold_in(key, 29), 2)
    bottom = jnp.clip(0.1 * jax.random.normal(subkeys[0], (NT, 1, S, S), jnp.float32), -0.4, 0.4)
    manning = jnp.exp(jax.random.uniform(subkeys[1], (NT, 1, S, S), jnp.float32, jnp.log(0.03), jnp.log(0.3)))
    return jnp.concatenate([bottom, manning], axis=1).astype(jnp.float32)


def setup_inputs(seed: int = 0, part: int = 0) -> dict:
    arg_keys = jax.random.split(jax.random.key(seed), 5)
    part_splits = jax.random.split(jax.random.fold_in(arg_keys[4], part), 5)
    return {
        "water_state": draw_water_state(jax.random.fold_in(jax.random.fold_in(arg_keys[4], part), 71), part),
        "terrain": draw_terrain(jax.random.fold_in(jax.random.fold_in(arg_keys[4], part), 71), part),
        "work_list": draw_work_list(jax.random.fold_in(jax.random.fold_in(arg_keys[4], part), 71), part),
        "edge_kind": draw_edge_kind(jax.random.fold_in(jax.random.fold_in(arg_keys[4], part), 71), part),
    }


GRAVITY = 9.81
DRY_DEPTH = 0.25
COURANT = 0.45

def wave_speed(grid_cells):
    floored = jnp.maximum(grid_cells[:, 0], DRY_DEPTH)
    return jnp.maximum(jnp.abs(grid_cells[:, 1]), jnp.abs(grid_cells[:, 2])) / floored + jnp.sqrt(GRAVITY * floored)

def ghost_rim(side_kinds, nearby, inside, normal):
    channel = jnp.arange(4, dtype=jnp.int32)[None, :, None]
    closed = side_kinds[:, None, None] == 0
    mirrored = jnp.where(closed & (channel == normal), -inside, inside)
    return jnp.where(side_kinds[:, None, None] == 1, nearby, mirrored)

def framed(grid_cells, north_ghost, south_ghost, west_ghost, east_ghost):
    middle = jnp.concatenate([north_ghost[:, :, None, :], grid_cells, south_ghost[:, :, None, :]], axis=2)
    left_column = jnp.pad(west_ghost, ((0, 0), (0, 0), (1, 1)))[..., None]
    right_column = jnp.pad(east_ghost, ((0, 0), (0, 0), (1, 1)))[..., None]
    return jnp.concatenate([left_column, middle, right_column], axis=3)

def advance(padded, manning, time_step):
    water_depth = padded[:, 0]
    flow_along = padded[:, 1]
    flow_across = padded[:, 2]
    bottom = padded[:, 3]
    floored = jnp.maximum(water_depth, DRY_DEPTH)
    pace_along = flow_along / floored
    pace_across = flow_across / floored
    celerity = jnp.sqrt(GRAVITY * floored)
    surface = water_depth + bottom
    pressure = 0.5 * GRAVITY * water_depth * water_depth
    left_face = (slice(None), slice(1, -1), slice(None, -1))
    right_face = (slice(None), slice(1, -1), slice(1, None))
    upper_face = (slice(None), slice(None, -1), slice(1, -1))
    lower_face = (slice(None), slice(1, None), slice(1, -1))
    centre = (slice(None), slice(1, -1), slice(1, -1))
    reach_along = jnp.maximum(jnp.abs(pace_along[left_face]) + celerity[left_face], jnp.abs(pace_along[right_face]) + celerity[right_face])
    mass_along = 0.5 * (flow_along[left_face] + flow_along[right_face]) - 0.5 * reach_along * (surface[right_face] - surface[left_face])
    first_along = 0.5 * (flow_along[left_face] * pace_along[left_face] + pressure[left_face] + flow_along[right_face] * pace_along[right_face] + pressure[right_face]) - 0.5 * reach_along * (flow_along[right_face] - flow_along[left_face])
    second_along = 0.5 * (flow_across[left_face] * pace_along[left_face] + flow_across[right_face] * pace_along[right_face]) - 0.5 * reach_along * (flow_across[right_face] - flow_across[left_face])
    reach_across = jnp.maximum(jnp.abs(pace_across[upper_face]) + celerity[upper_face], jnp.abs(pace_across[lower_face]) + celerity[lower_face])
    mass_across = 0.5 * (flow_across[upper_face] + flow_across[lower_face]) - 0.5 * reach_across * (surface[lower_face] - surface[upper_face])
    first_across = 0.5 * (flow_along[upper_face] * pace_across[upper_face] + flow_along[lower_face] * pace_across[lower_face]) - 0.5 * reach_across * (flow_along[lower_face] - flow_along[upper_face])
    second_across = 0.5 * (flow_across[upper_face] * pace_across[upper_face] + pressure[upper_face] + flow_across[lower_face] * pace_across[lower_face] + pressure[lower_face]) - 0.5 * reach_across * (flow_across[lower_face] - flow_across[upper_face])
    depth_centre = water_depth[centre]
    along_centre = flow_along[centre]
    across_centre = flow_across[centre]
    new_depth = depth_centre - time_step * (mass_along[:, :, 1:] - mass_along[:, :, :-1] + (mass_across[:, 1:, :] - mass_across[:, :-1, :]))
    moved_along = along_centre - time_step * (first_along[:, :, 1:] - first_along[:, :, :-1] + (first_across[:, 1:, :] - first_across[:, :-1, :])) - time_step * GRAVITY * depth_centre * 0.5 * (bottom[:, 1:-1, 2:] - bottom[:, 1:-1, :-2])
    moved_across = across_centre - time_step * (second_along[:, :, 1:] - second_along[:, :, :-1] + (second_across[:, 1:, :] - second_across[:, :-1, :])) - time_step * GRAVITY * depth_centre * 0.5 * (bottom[:, 2:, 1:-1] - bottom[:, :-2, 1:-1])
    floor_centre = jnp.maximum(depth_centre, DRY_DEPTH)
    magnitude = jnp.sqrt(along_centre * along_centre + across_centre * across_centre)
    damping = 1.0 + time_step * GRAVITY * manning * manning * magnitude / floor_centre ** (7.0 / 3.0)
    return jnp.stack([new_depth, moved_along / damping, moved_across / damping], axis=1)

def neighbours(tile_ids, count_tiles):
    return (jnp.maximum(tile_ids - TW, 0), jnp.minimum(tile_ids + TW, count_tiles - 1), jnp.maximum(tile_ids - 1, 0), jnp.minimum(tile_ids + 1, count_tiles - 1))

def reference(water_state, terrain, work_list, edge_kind):
    listed = work_list.shape[0]
    active = work_list < NT
    chosen = jnp.minimum(work_list, NT - 1)
    side_kinds = jnp.where(active[:, None], edge_kind[chosen], 0)
    places = jnp.zeros((NT,), jnp.int32).at[work_list].set(jnp.arange(listed, dtype=jnp.int32), mode='drop')
    north_at, south_at, west_at, east_at = [places[nearby_ids] for nearby_ids in neighbours(chosen, NT)]
    grid_cells = jnp.concatenate([water_state[chosen], terrain[chosen, 0:1]], axis=1)
    manning = terrain[chosen, 1]
    for iteration in range(ITERS):
        speeds = jnp.where(active[:, None, None], wave_speed(grid_cells), 0.0)
        time_step = COURANT / jnp.max(speeds)
        north_ghost = ghost_rim(side_kinds[:, 0], grid_cells[:, :, S - 1, :][north_at], grid_cells[:, :, 0, :], 2)
        south_ghost = ghost_rim(side_kinds[:, 1], grid_cells[:, :, 0, :][south_at], grid_cells[:, :, S - 1, :], 2)
        west_ghost = ghost_rim(side_kinds[:, 2], grid_cells[:, :, :, S - 1][west_at], grid_cells[:, :, :, 0], 1)
        east_ghost = ghost_rim(side_kinds[:, 3], grid_cells[:, :, :, 0][east_at], grid_cells[:, :, :, S - 1], 1)

        def advance_one(pieces, time_step=time_step):
            entry_cells, upper_rim, lower_rim, left_rim, right_rim, roughness = pieces
            padded = framed(entry_cells[None], upper_rim[None], lower_rim[None], left_rim[None], right_rim[None])
            return advance(padded, roughness[None], time_step)[0]
        updated = lax.map(advance_one, (grid_cells, north_ghost, south_ghost, west_ghost, east_ghost, manning))
        grid_cells = jnp.concatenate([updated, grid_cells[:, 3:4]], axis=1)
    return water_state.at[work_list].set(grid_cells[:, :3], mode='drop')
```

```python
import functools

import jax
import jax.numpy as jnp
from jax import lax
from jax.experimental import pallas as pl
from jax.experimental.pallas import tpu as pltpu
from jax.sharding import PartitionSpec as P

TW = 16
ITERS = 4


GRAVITY = 9.81
DRY_DEPTH = 0.25
COURANT = 0.45


def roll_rows(x, shift):
    rows = x.shape[0]
    if rows % 8 == 0:
        return pltpu.roll(x, shift % rows, 0)
    cut = (rows - shift) % rows
    return jnp.concatenate([x[cut:], x[:cut]], axis=0)


def roll_lanes(x, shift):
    return pltpu.roll(x, shift % x.shape[1], 1)


def face(left, right):
    reach = jnp.maximum(left[1], right[1])
    mass = (left[0] + right[0]) - reach * (right[2] - left[2])
    first = (left[3] + right[3]) - reach * (right[0] - left[0])
    second = (left[4] + right[4]) - reach * (right[5] - left[5])
    return mass, first, second


def speeds(h, p, q):
    floored = jnp.maximum(h, DRY_DEPTH)
    inverse = 1.0 / floored
    scaled = GRAVITY * floored
    return p * inverse, q * inverse, scaled * lax.rsqrt(scaled), floored


def stepper(n, work, kinds, water, terrain, state, wv, tv, zs, rough, slope_x, slope_y, pace, derived,
            tend, rows_out, rows_in, z_out, z_in, ghost, ghost_z, landed, edge, edge_kinds, top_out, top_in,
            near, local_sem, top_send, top_recv, row_send, row_recv, z_send, z_recv):
    count_tiles = water.shape[0]
    listed = state.shape[0]
    rows, width = state.shape[2], state.shape[3]
    half = width // 2
    me = lax.axis_index("tiles")
    at_first = me == 0
    at_final = me == n - 1

    barrier = pltpu.get_barrier_semaphore()
    for d in range(1, n):
        pl.semaphore_signal(
            barrier, inc=1, device_id={"tiles": lax.rem(me + d, n)}, device_id_type=pl.DeviceIdType.MESH
        )
    water_in = pltpu.make_async_copy(water, wv, local_sem.at[0])
    terrain_in = pltpu.make_async_copy(terrain, tv, local_sem.at[1])
    water_in.start()
    terrain_in.start()

    entries = [work[j] for j in range(listed)]

    def locate(s, carry):
        tile = work[s]
        chosen = jnp.minimum(tile, count_tiles - 1)
        active = tile < count_tiles
        found = [jnp.int32(0)] * 4
        sides = (chosen - TW, chosen + TW, chosen - 1, chosen + 1)
        for j in range(listed):
            found = [jnp.where(entries[j] == side, j, f) for side, f in zip(sides, found)]
        for e in range(4):
            near[e, s] = found[e]
            kind = jnp.where(active, kinds[chosen, e], 0)
            near[4 + e, s] = kind
            if e < 2:
                outer = jnp.where(at_first if e == 0 else at_final, kind, 1)
                edge_kinds[e, pl.ds(s, 1), :] = jnp.full((1, width), outer, jnp.int32)
        return carry

    lax.fori_loop(0, listed, locate, 0)

    row_at = lax.broadcasted_iota(jnp.int32, (rows, width), 0)
    lane_at = lax.broadcasted_iota(jnp.int32, (rows, half), 1)
    inner = row_at < rows - 1

    def settle(s, k, h, p, q, top):
        u, v, c, _ = speeds(h, p, q)
        for i, x in enumerate((h, p, q)):
            state[s, i] = x
            rows_out[k, 0, i, pl.ds(s, 1), :] = x[:1]
            rows_out[k, 1, i, pl.ds(s, 1), :] = x[rows - 1 :]
        for i, x in enumerate((u, v, c)):
            pace[s, i] = x
        fastest = jnp.maximum(jnp.abs(u), jnp.abs(v)) + c
        return jnp.maximum(top, jnp.where(work[s] < count_tiles, fastest, 0.0))

    def publish(k, top):
        part = jnp.max(top, axis=0, keepdims=True)
        top_out[k] = jnp.maximum(part[:, :half], part[:, half:])

    water_in.wait()
    terrain_in.wait()

    def gather(s, top):
        chosen = jnp.minimum(work[s], count_tiles - 1)
        z = tv[chosen, 0]
        zs[s] = z
        z_out[0, pl.ds(s, 1), :] = z[:1]
        z_out[1, pl.ds(s, 1), :] = z[rows - 1 :]
        return settle(s, 0, wv[chosen, 0], wv[chosen, 1], wv[chosen, 2], top)

    publish(0, lax.fori_loop(0, listed, gather, jnp.zeros((rows, width), jnp.float32)))
    pl.semaphore_wait(barrier, n - 1)

    up = {"tiles": lax.rem(me + n - 1, n)}
    down = {"tiles": lax.rem(me + 1, n)}

    def remote(src, dst, send, recv, to):
        return pltpu.make_async_remote_copy(
            src_ref=src, dst_ref=dst, send_sem=send, recv_sem=recv, device_id=to,
            device_id_type=pl.DeviceIdType.MESH,
        )

    def top_copies(k):
        return [
            remote(top_out.at[k], top_in.at[k, d - 1], top_send.at[k, d - 1], top_recv.at[k, d - 1],
                   {"tiles": lax.rem(me + d, n)})
            for d in range(1, n)
        ]

    def row_copies(k):
        return [
            remote(rows_out.at[k, 0], rows_in.at[k, 1], row_send.at[k, 0], row_recv.at[k, 1], up),
            remote(rows_out.at[k, 1], rows_in.at[k, 0], row_send.at[k, 1], row_recv.at[k, 0], down),
        ]

    z_copies = [
        remote(z_out.at[0], z_in.at[1], z_send.at[0], z_recv.at[1], up),
        remote(z_out.at[1], z_in.at[0], z_send.at[1], z_recv.at[0], down),
    ]

    def prepare(s, carry):
        chosen = jnp.minimum(work[s], count_tiles - 1)
        z = zs[s]
        manning = tv[chosen, 1]
        rough[s] = (2.0 * GRAVITY) * manning * manning
        west_z = zs[near[2, s]][:, half:]
        east_z = zs[near[3, s]][:, :half]
        west_open = near[6, s] == 1
        east_open = near[7, s] == 1
        z_low, z_high = z[:, :half], z[:, half:]
        to_east = roll_lanes(z, -1)
        to_west = roll_lanes(z, 1)
        last = jnp.where(east_open, roll_lanes(east_z, -1), z_high)
        first = jnp.where(west_open, roll_lanes(west_z, 1), z_low)
        east = jnp.concatenate([to_east[:, :half], jnp.where(lane_at == half - 1, last, to_east[:, half:])], axis=1)
        west = jnp.concatenate([jnp.where(lane_at == 0, first, to_west[:, :half]), to_west[:, half:]], axis=1)
        slope_x[s] = GRAVITY * (east - west)
        south = jnp.where(inner, roll_rows(z, -1), 0.0)
        north = jnp.where(row_at == 0, 0.0, roll_rows(z, 1))
        slope_y[s] = GRAVITY * (south - north)
        return carry

    def derive(s, carry):
        h, p, q = state[s, 0], state[s, 1], state[s, 2]
        u, v, c = pace[s, 0], pace[s, 1], pace[s, 2]
        pressure = (0.5 * GRAVITY) * h * h
        derived[s, 0] = jnp.abs(u) + c
        derived[s, 1] = h + zs[s]
        derived[s, 2] = p * u + pressure
        derived[s, 3] = q * u
        derived[s, 4] = jnp.abs(v) + c
        derived[s, 5] = q * v + pressure
        floored = jnp.maximum(h, DRY_DEPTH)
        resist = jnp.exp2(jnp.log2(floored) * (-7.0 / 3.0))
        tend[s, 3] = rough[s] * jnp.sqrt(p * p + q * q) * resist
        return carry

    def along(s, lanes):
        return (state[s, 1, :, lanes], derived[s, 0, :, lanes], derived[s, 1, :, lanes],
                derived[s, 2, :, lanes], derived[s, 3, :, lanes], state[s, 2, :, lanes])

    low, high, whole = pl.ds(0, half), pl.ds(half, half), pl.ds(0, width)

    def balance(s, carry):
        own = along(s, whole)
        own_low = [x[:, :half] for x in own]
        own_high = [x[:, half:] for x in own]
        from_west = along(near[2, s], high)
        from_east = along(near[3, s], low)
        west_kind, east_kind = near[6, s], near[7, s]

        beyond = [
            roll_lanes(jnp.concatenate([jnp.where(lane_at == 0, g, a), b], axis=1), -1)
            for g, a, b in zip(from_east, own_low, own_high)
        ]
        flux = face(own, beyond)
        closed = 2.0 * own_high[1] * own_high[0]
        shut = (
            jnp.where(east_kind == 2, 2.0 * own_high[0], 0.0),
            2.0 * own_high[3] + jnp.where(east_kind == 0, closed, 0.0),
            jnp.where(east_kind == 2, 2.0 * own_high[4], 0.0),
        )
        rim = (lane_at == half - 1) & (east_kind != 1)
        flux = [
            jnp.concatenate([f[:, :half], jnp.where(rim, g, f[:, half:])], axis=1) for f, g in zip(flux, shut)
        ]
        entry = face([roll_lanes(x, 1) for x in from_west], own_low)
        closed = 2.0 * own_low[1] * own_low[0]
        shut = (
            jnp.where(west_kind == 2, 2.0 * own_low[0], 0.0),
            2.0 * own_low[3] - jnp.where(west_kind == 0, closed, 0.0),
            jnp.where(west_kind == 2, 2.0 * own_low[4], 0.0),
        )
        entry = [jnp.where(west_kind == 1, f, g) for f, g in zip(entry, shut)]
        change = []
        for f, g in zip(flux, entry):
            back = roll_lanes(f, 1)
            back = jnp.concatenate([jnp.where(lane_at == 0, g, back[:, :half]), back[:, half:]], axis=1)
            change.append(f - back)

        column = (own[5], derived[s, 4], own[2], derived[s, 5], own[4], own[0])
        flux = face(column, [roll_rows(x, -1) for x in column])
        flux = [jnp.where(inner, f, 0.0) for f in flux]
        across = [f - roll_rows(f, 1) for f in flux]
        h = state[s, 0]
        tend[s, 0] = change[0] + across[0]
        tend[s, 1] = change[1] + across[2] + h * slope_x[s]
        tend[s, 2] = change[2] + across[1] + h * slope_y[s]
        return carry

    def place_rows(side, source, target, channels):
        at_rim = at_first if side == 0 else at_final

        @pl.when(at_rim)
        def _():
            for i, index in enumerate(channels):
                landed[i] = source[index + (slice(None), slice(None))]

            def one(s, carry):
                nearby = near[side, s]
                for i, index in enumerate(channels):
                    target[(side,) + index + (pl.ds(s, 1), slice(None))] = landed[i, pl.ds(nearby, 1), :]
                return carry

            lax.fori_loop(0, listed, one, 0)

        @pl.when(jnp.logical_not(at_rim))
        def _():
            target[side] = source[...]

    def rim_cells(h, p, q, z):
        u, v, c, _ = speeds(h, p, q)
        return (q, jnp.abs(v) + c, h + z, q * v + (0.5 * GRAVITY) * h * h, q * u, p)

    def rim(k, side):
        open_edge = edge_kinds[side] == 1
        wall = edge_kinds[side] == 0
        h, p, q, z = rows_out[k, side, 0], rows_out[k, side, 1], rows_out[k, side, 2], z_out[side]
        gh = jnp.where(open_edge, ghost[side, 0], h)
        gp = jnp.where(open_edge, ghost[side, 1], p)
        gq = jnp.where(open_edge, ghost[side, 2], jnp.where(wall, -q, q))
        gz = jnp.where(open_edge, ghost_z[side], z)
        mine, theirs = rim_cells(h, p, q, z), rim_cells(gh, gp, gq, gz)
        mass, first, second = face(theirs, mine) if side == 0 else face(mine, theirs)
        sign = -1.0 if side == 0 else 1.0
        edge[side, 0] = sign * mass
        edge[side, 1] = sign * second
        edge[side, 2] = sign * (first + GRAVITY * h * gz)

    def close_rows(s, carry):
        for i in range(3):
            tend[s, i, :1] += edge[0, i, pl.ds(s, 1), :]
            tend[s, i, rows - 1 :] += edge[1, i, pl.ds(s, 1), :]
        return carry

    def step(k, carry):
        tops, halos = top_copies(k), row_copies(k)
        for copy in tops:
            copy.start()
        for copy in halos:
            copy.start()

        @pl.when(k == 0)
        def _():
            for copy in z_copies:
                copy.start()
            lax.fori_loop(0, listed, prepare, 0)

        lax.fori_loop(0, listed, derive, 0)
        lax.fori_loop(0, listed, balance, 0)

        @pl.when(k == 0)
        def _():
            for copy in z_copies:
                copy.wait()
            for side in range(2):
                place_rows(side, z_in.at[side], ghost_z, [()])

        for copy in halos:
            copy.wait()
        for side in range(2):
            place_rows(side, rows_in.at[k, side], ghost, [(0,), (1,), (2,)])
            rim(k, side)
        lax.fori_loop(0, listed, close_rows, 0)

        for copy in tops:
            copy.wait()
        top = jnp.maximum(jnp.max(top_in[k], axis=0), top_out[k])
        top = jnp.max(top, axis=1, keepdims=True)
        span = jnp.broadcast_to((COURANT / top) * 0.5, (rows, width))

        def update(s, top):
            h = state[s, 0] - span * tend[s, 0]
            damping = 1.0 / (1.0 + span * tend[s, 3])
            p = (state[s, 1] - span * tend[s, 1]) * damping
            q = (state[s, 2] - span * tend[s, 2]) * damping
            return settle(s, k + 1, h, p, q, top)

        publish(k + 1, lax.fori_loop(0, listed, update, jnp.zeros((rows, width), jnp.float32)))
        return carry

    lax.fori_loop(0, ITERS, step, 0)


def writer(work, water, stepped, out, owner, sem):
    count_tiles = water.shape[0]
    for t in range(count_tiles + 1):
        owner[t] = -1
    for s in range(work.shape[0]):
        owner[work[s]] = s

    def one(t, carry):
        slot = owner[t]

        @pl.when(slot >= 0)
        def _():
            pltpu.make_async_copy(stepped.at[slot], out.at[t], sem).start()

        @pl.when(slot < 0)
        def _():
            pltpu.make_async_copy(water.at[t], out.at[t], sem).start()

        return carry

    lax.fori_loop(0, count_tiles, one, 0)
    pltpu.make_async_copy(water, out, sem).wait()


def body(n, water_state, terrain, work_list, edge_kind):
    count_tiles, _, rows, width = water_state.shape
    listed = work_list.shape[0]
    smem = pl.BlockSpec(memory_space=pltpu.SMEM)
    anywhere = pl.BlockSpec(memory_space=pl.ANY)
    f32 = jnp.float32

    def vmem(*shape, dtype=f32):
        return pltpu.VMEM(shape, dtype)

    dma = pltpu.SemaphoreType.DMA
    stepped = pl.pallas_call(
        functools.partial(stepper, n),
        out_shape=jax.ShapeDtypeStruct((listed, 3, rows, width), f32),
        in_specs=[smem, smem, anywhere, anywhere],
        out_specs=pl.BlockSpec(memory_space=pltpu.VMEM),
        scratch_shapes=[
            vmem(count_tiles, 3, rows, width),
            vmem(count_tiles, 2, rows, width),
            vmem(listed, rows, width),
            vmem(listed, rows, width),
            vmem(listed, rows, width),
            vmem(listed, rows, width),
            vmem(listed, 3, rows, width),
            vmem(listed, 6, rows, width),
            vmem(listed, 4, rows, width),
            vmem(ITERS + 1, 2, 3, listed, width),
            vmem(ITERS, 2, 3, listed, width),
            vmem(2, listed, width),
            vmem(2, listed, width),
            vmem(2, 3, listed, width),
            vmem(2, listed, width),
            vmem(3, listed, width),
            vmem(2, 3, listed, width),
            vmem(2, listed, width, dtype=jnp.int32),
            vmem(ITERS + 1, 1, width // 2),
            vmem(ITERS, n - 1, 1, width // 2),
            pltpu.SMEM((8, listed), jnp.int32),
            dma((2,)),
            dma((ITERS, n - 1)),
            dma((ITERS, n - 1)),
            dma((ITERS, 2)),
            dma((ITERS, 2)),
            dma((2,)),
            dma((2,)),
        ],
        compiler_params=pltpu.CompilerParams(
            collective_id=0, has_side_effects=True, vmem_limit_bytes=48 * 1024 * 1024
        ),
    )(work_list, edge_kind, water_state, terrain)
    return pl.pallas_call(
        writer,
        out_shape=jax.ShapeDtypeStruct(water_state.shape, f32),
        in_specs=[smem, anywhere, anywhere],
        out_specs=anywhere,
        scratch_shapes=[pltpu.SMEM((count_tiles + 1,), jnp.int32), pltpu.SemaphoreType.DMA],
    )(work_list, water_state, stepped)


def solution(mesh):
    placed = (
        P("groups", None, "tiles", None),
        P("groups", None, "tiles", None),
        P("groups"),
        P("groups", None),
    )
    return jax.shard_map(
        functools.partial(body, mesh.shape["tiles"]),
        mesh=mesh,
        in_specs=placed,
        out_specs=P("groups", None, "tiles", None),
        check_vma=False,
    )
```

```python
import functools

import jax
import jax.numpy as jnp
from jax import lax
from jax.experimental import pallas as pl
from jax.experimental.pallas import tpu as pltpu
from jax.sharding import PartitionSpec as P

TW = 16
ITERS = 4


GRAVITY = 9.81
DRY_DEPTH = 0.25
COURANT = 0.45


def roll_rows(x, shift):
    rows = x.shape[0]
    if rows % 8 == 0:
        return pltpu.roll(x, shift % rows, 0)
    cut = (rows - shift) % rows
    return jnp.concatenate([x[cut:], x[:cut]], axis=0)


def roll_lanes(x, shift):
    return pltpu.roll(x, shift % x.shape[1], 1)


def face(left, right):
    reach = jnp.maximum(left[1], right[1])
    mass = (left[0] + right[0]) - reach * (right[2] - left[2])
    first = (left[3] + right[3]) - reach * (right[0] - left[0])
    second = (left[4] + right[4]) - reach * (right[5] - left[5])
    return mass, first, second


def speeds(h, p, q):
    floored = jnp.maximum(h, DRY_DEPTH)
    root = lax.rsqrt(floored)
    inverse = root * root
    return p * inverse, q * inverse, (GRAVITY**0.5) * (floored * root)


def stepper(n, work, kinds, water, terrain, out, state, wv, tv, zs, rough, slope_x, slope_y, pace, derived,
            tend, rows_out, rows_in, z_out, z_in, ghost, ghost_z, landed, edge, edge_kinds, top_out, top_in,
            near, owner, local_sem, top_send, top_recv, row_send, row_recv, z_send, z_recv):
    count_tiles = water.shape[0]
    listed = state.shape[0]
    rows, width = state.shape[2], state.shape[3]
    half = width // 2
    me = lax.axis_index("tiles")
    at_first = me == 0
    at_final = me == n - 1

    barrier = pltpu.get_barrier_semaphore()
    for d in range(1, n):
        pl.semaphore_signal(
            barrier, inc=1, device_id={"tiles": lax.rem(me + d, n)}, device_id_type=pl.DeviceIdType.MESH
        )
    water_in = pltpu.make_async_copy(water, wv, local_sem.at[0])
    terrain_in = pltpu.make_async_copy(terrain, tv, local_sem.at[1])
    water_in.start()
    terrain_in.start()

    entries = [work[j] for j in range(listed)]

    def locate(s, carry):
        tile = work[s]
        chosen = jnp.minimum(tile, count_tiles - 1)
        active = tile < count_tiles
        found = [jnp.int32(0)] * 4
        sides = (chosen - TW, chosen + TW, chosen - 1, chosen + 1)
        for j in range(listed):
            found = [jnp.where(entries[j] == side, j, f) for side, f in zip(sides, found)]
        for e in range(4):
            near[e, s] = found[e]
            kind = jnp.where(active, kinds[e, chosen], 0)
            near[4 + e, s] = kind
            if e < 2:
                outer = jnp.where(at_first if e == 0 else at_final, kind, 1)
                edge_kinds[e, pl.ds(s, 1), :] = jnp.full((1, width), outer, jnp.int32)
        return carry

    lax.fori_loop(0, listed, locate, 0)

    def slots(one, unroll, carry=0):
        unroll = unroll if listed % unroll == 0 else 1

        def several(i, carry):
            for j in range(unroll):
                carry = one(i * unroll + j, carry)
            return carry

        return lax.fori_loop(0, listed // unroll, several, carry)

    row_at = lax.broadcasted_iota(jnp.int32, (rows, width), 0)
    lane_at = lax.broadcasted_iota(jnp.int32, (rows, half), 1)
    inner = row_at < rows - 1

    def settle(s, size, k, h, p, q, top):
        u, v, c = speeds(h, p, q)
        block = pl.ds(s, size)
        for i, x in enumerate((h, p, q)):
            state[block, i] = x
            for j in range(size):
                rows_out[k, 0, i, pl.ds(s + j, 1), :] = x[j, :1]
                rows_out[k, 1, i, pl.ds(s + j, 1), :] = x[j, rows - 1 :]
        for i, x in enumerate((u, v, c)):
            pace[block, i] = x
        fastest = jnp.maximum(jnp.abs(u), jnp.abs(v)) + c
        for j in range(size):
            top = jnp.maximum(top, jnp.where(work[s + j] < count_tiles, fastest[j], 0.0))
        return top

    def publish(k, top):
        part = jnp.max(top, axis=0, keepdims=True)
        top_out[k] = jnp.maximum(part[:, :half], part[:, half:])

    water_in.wait()
    terrain_in.wait()

    def gather(s, top):
        chosen = jnp.minimum(work[s], count_tiles - 1)
        z = tv[chosen, 0]
        zs[s] = z
        z_out[0, pl.ds(s, 1), :] = z[:1]
        z_out[1, pl.ds(s, 1), :] = z[rows - 1 :]
        return settle(s, 1, 0, *[wv[pl.ds(chosen, 1), i] for i in range(3)], top)

    publish(0, slots(gather, 2, jnp.zeros((rows, width), jnp.float32)))
    pl.semaphore_wait(barrier, n - 1)

    up = {"tiles": lax.rem(me + n - 1, n)}
    down = {"tiles": lax.rem(me + 1, n)}

    def remote(src, dst, send, recv, to):
        return pltpu.make_async_remote_copy(
            src_ref=src, dst_ref=dst, send_sem=send, recv_sem=recv, device_id=to,
            device_id_type=pl.DeviceIdType.MESH,
        )

    def top_copies(k):
        return [
            remote(top_out.at[k], top_in.at[k, d - 1], top_send.at[k, d - 1], top_recv.at[k, d - 1],
                   {"tiles": lax.rem(me + d, n)})
            for d in range(1, n)
        ]

    def row_copies(k):
        return [
            remote(rows_out.at[k, 0], rows_in.at[k, 1], row_send.at[k, 0], row_recv.at[k, 1], up),
            remote(rows_out.at[k, 1], rows_in.at[k, 0], row_send.at[k, 1], row_recv.at[k, 0], down),
        ]

    z_copies = [
        remote(z_out.at[0], z_in.at[1], z_send.at[0], z_recv.at[1], up),
        remote(z_out.at[1], z_in.at[0], z_send.at[1], z_recv.at[0], down),
    ]

    def prepare(s, carry):
        chosen = jnp.minimum(work[s], count_tiles - 1)
        z = zs[s]
        manning = tv[chosen, 1]
        rough[s] = (2.0 * GRAVITY) * manning * manning
        west_z = zs[near[2, s]][:, half:]
        east_z = zs[near[3, s]][:, :half]
        west_open = near[6, s] == 1
        east_open = near[7, s] == 1
        z_low, z_high = z[:, :half], z[:, half:]
        to_east = roll_lanes(z, -1)
        to_west = roll_lanes(z, 1)
        last = jnp.where(east_open, roll_lanes(east_z, -1), z_high)
        first = jnp.where(west_open, roll_lanes(west_z, 1), z_low)
        east = jnp.concatenate([to_east[:, :half], jnp.where(lane_at == half - 1, last, to_east[:, half:])], axis=1)
        west = jnp.concatenate([jnp.where(lane_at == 0, first, to_west[:, :half]), to_west[:, half:]], axis=1)
        slope_x[s] = GRAVITY * (east - west)
        south = jnp.where(inner, roll_rows(z, -1), 0.0)
        north = jnp.where(row_at == 0, 0.0, roll_rows(z, 1))
        slope_y[s] = GRAVITY * (south - north)
        share = -(-count_tiles // listed)
        for j in range(share):
            tile = jnp.minimum(s * share + j, count_tiles - 1)
            slot = jnp.int32(-1)
            for i in range(listed):
                slot = jnp.where(entries[i] == tile, i, slot)
            owner[tile] = slot
        return carry

    size = next(d for d in (4, 2, 1) if listed % d == 0)

    def derive(i, carry):
        block = pl.ds(i * size, size)
        h, p, q = state[block, 0], state[block, 1], state[block, 2]
        u, v, c = pace[block, 0], pace[block, 1], pace[block, 2]
        pressure = (0.5 * GRAVITY) * h * h
        derived[block, 0] = jnp.abs(u) + c
        derived[block, 1] = h + zs[block]
        derived[block, 2] = p * u + pressure
        derived[block, 3] = q * u
        derived[block, 4] = jnp.abs(v) + c
        derived[block, 5] = q * v + pressure
        floored = jnp.maximum(h, DRY_DEPTH)
        resist = jnp.exp2(jnp.log2(floored) * (-7.0 / 3.0))
        tend[block, 3] = rough[block] * jnp.sqrt(p * p + q * q) * resist
        return carry

    def along(s, lanes):
        return (state[s, 1, :, lanes], derived[s, 0, :, lanes], derived[s, 1, :, lanes],
                derived[s, 2, :, lanes], derived[s, 3, :, lanes], state[s, 2, :, lanes])

    low, high, whole = pl.ds(0, half), pl.ds(half, half), pl.ds(0, width)

    def balance(s, carry):
        own = along(s, whole)
        own_low = [x[:, :half] for x in own]
        own_high = [x[:, half:] for x in own]
        from_west = along(near[2, s], high)
        from_east = along(near[3, s], low)
        west_kind, east_kind = near[6, s], near[7, s]

        beyond = [
            roll_lanes(jnp.concatenate([jnp.where(lane_at == 0, g, a), b], axis=1), -1)
            for g, a, b in zip(from_east, own_low, own_high)
        ]
        flux = face(own, beyond)
        closed = 2.0 * own_high[1] * own_high[0]
        shut = (
            jnp.where(east_kind == 2, 2.0 * own_high[0], 0.0),
            2.0 * own_high[3] + jnp.where(east_kind == 0, closed, 0.0),
            jnp.where(east_kind == 2, 2.0 * own_high[4], 0.0),
        )
        rim = (lane_at == half - 1) & (east_kind != 1)
        flux = [
            jnp.concatenate([f[:, :half], jnp.where(rim, g, f[:, half:])], axis=1) for f, g in zip(flux, shut)
        ]
        entry = face([roll_lanes(x, 1) for x in from_west], own_low)
        closed = 2.0 * own_low[1] * own_low[0]
        shut = (
            jnp.where(west_kind == 2, 2.0 * own_low[0], 0.0),
            2.0 * own_low[3] - jnp.where(west_kind == 0, closed, 0.0),
            jnp.where(west_kind == 2, 2.0 * own_low[4], 0.0),
        )
        entry = [jnp.where(west_kind == 1, f, g) for f, g in zip(entry, shut)]
        change = []
        for f, g in zip(flux, entry):
            back = roll_lanes(f, 1)
            back = jnp.concatenate([jnp.where(lane_at == 0, g, back[:, :half]), back[:, half:]], axis=1)
            change.append(f - back)

        column = (own[5], derived[s, 4], own[2], derived[s, 5], own[4], own[0])
        flux = face(column, [roll_rows(x, -1) for x in column])
        flux = [jnp.where(inner, f, 0.0) for f in flux]
        across = [f - roll_rows(f, 1) for f in flux]
        h = state[s, 0]
        tend[s, 0] = change[0] + across[0]
        tend[s, 1] = change[1] + across[2] + h * slope_x[s]
        tend[s, 2] = change[2] + across[1] + h * slope_y[s]
        return carry

    def place_rows(side, source, target, channels):
        at_rim = at_first if side == 0 else at_final

        @pl.when(at_rim)
        def _():
            for i, index in enumerate(channels):
                landed[i] = source[index + (slice(None), slice(None))]

            def one(s, carry):
                nearby = near[side, s]
                for i, index in enumerate(channels):
                    target[(side,) + index + (pl.ds(s, 1), slice(None))] = landed[i, pl.ds(nearby, 1), :]
                return carry

            lax.fori_loop(0, listed, one, 0)

        @pl.when(jnp.logical_not(at_rim))
        def _():
            target[side] = source[...]

    def rim_cells(h, p, q, z):
        u, v, c = speeds(h, p, q)
        return (q, jnp.abs(v) + c, h + z, q * v + (0.5 * GRAVITY) * h * h, q * u, p)

    def rim(k, side):
        open_edge = edge_kinds[side] == 1
        wall = edge_kinds[side] == 0
        h, p, q, z = rows_out[k, side, 0], rows_out[k, side, 1], rows_out[k, side, 2], z_out[side]
        gh = jnp.where(open_edge, ghost[side, 0], h)
        gp = jnp.where(open_edge, ghost[side, 1], p)
        gq = jnp.where(open_edge, ghost[side, 2], jnp.where(wall, -q, q))
        gz = jnp.where(open_edge, ghost_z[side], z)
        mine, theirs = rim_cells(h, p, q, z), rim_cells(gh, gp, gq, gz)
        mass, first, second = face(theirs, mine) if side == 0 else face(mine, theirs)
        sign = -1.0 if side == 0 else 1.0
        edge[side, 0] = sign * mass
        edge[side, 1] = sign * second
        edge[side, 2] = sign * (first + GRAVITY * h * gz)

    def close_rows(s, carry):
        for i in range(3):
            tend[s, i, :1] += edge[0, i, pl.ds(s, 1), :]
            tend[s, i, rows - 1 :] += edge[1, i, pl.ds(s, 1), :]
        return carry

    def step(k, carry):
        tops, halos = top_copies(k), row_copies(k)
        for copy in tops:
            copy.start()
        for copy in halos:
            copy.start()

        @pl.when(k == 0)
        def _():
            for copy in z_copies:
                copy.start()
            slots(prepare, 2)

        lax.fori_loop(0, listed // size, derive, 0)
        slots(balance, 2)

        @pl.when(k == 0)
        def _():
            for copy in z_copies:
                copy.wait()
            for side in range(2):
                place_rows(side, z_in.at[side], ghost_z, [()])

        for copy in halos:
            copy.wait()
        for side in range(2):
            place_rows(side, rows_in.at[k, side], ghost, [(0,), (1,), (2,)])
            rim(k, side)
        slots(close_rows, 4)

        for copy in tops:
            copy.wait()
        top = jnp.maximum(jnp.max(top_in[k], axis=0), top_out[k])
        top = jnp.max(top, axis=1, keepdims=True)
        span = jnp.broadcast_to((COURANT / top) * 0.5, (rows, width))

        def update(i, top):
            block = pl.ds(i * size, size)
            h = state[block, 0] - span * tend[block, 0]
            root = lax.rsqrt(1.0 + span * tend[block, 3])
            damping = root * root
            p = (state[block, 1] - span * tend[block, 1]) * damping
            q = (state[block, 2] - span * tend[block, 2]) * damping
            return settle(i * size, size, k + 1, h, p, q, top)

        publish(k + 1, lax.fori_loop(0, listed // size, update, jnp.zeros((rows, width), jnp.float32)))
        return carry

    lax.fori_loop(0, ITERS, step, 0)

    def merge(t, carry):
        slot = owner[t]
        out[t] = jnp.where(slot >= 0, state[jnp.maximum(slot, 0)], wv[t])
        return carry

    lax.fori_loop(0, count_tiles, merge, 0)


def body(n, water_state, terrain, work_list, edge_kind):
    count_tiles, _, rows, width = water_state.shape
    listed = work_list.shape[0]
    smem = pl.BlockSpec(memory_space=pltpu.SMEM)
    anywhere = pl.BlockSpec(memory_space=pltpu.HBM)
    f32 = jnp.float32

    def vmem(*shape, dtype=f32):
        return pltpu.VMEM(shape, dtype)

    dma = pltpu.SemaphoreType.DMA
    return pl.pallas_call(
        functools.partial(stepper, n),
        out_shape=jax.ShapeDtypeStruct(water_state.shape, f32),
        in_specs=[smem, smem, anywhere, anywhere],
        out_specs=pl.BlockSpec(memory_space=pltpu.VMEM),
        scratch_shapes=[
            vmem(listed, 3, rows, width),
            vmem(count_tiles, 3, rows, width),
            vmem(count_tiles, 2, rows, width),
            vmem(listed, rows, width),
            vmem(listed, rows, width),
            vmem(listed, rows, width),
            vmem(listed, rows, width),
            vmem(listed, 3, rows, width),
            vmem(listed, 6, rows, width),
            vmem(listed, 4, rows, width),
            vmem(ITERS + 1, 2, 3, listed, width),
            vmem(ITERS, 2, 3, listed, width),
            vmem(2, listed, width),
            vmem(2, listed, width),
            vmem(2, 3, listed, width),
            vmem(2, listed, width),
            vmem(3, listed, width),
            vmem(2, 3, listed, width),
            vmem(2, listed, width, dtype=jnp.int32),
            vmem(ITERS + 1, 1, width // 2),
            vmem(ITERS, n - 1, 1, width // 2),
            pltpu.SMEM((8, listed), jnp.int32),
            pltpu.SMEM((count_tiles,), jnp.int32),
            dma((2,)),
            dma((ITERS, n - 1)),
            dma((ITERS, n - 1)),
            dma((ITERS, 2)),
            dma((ITERS, 2)),
            dma((2,)),
            dma((2,)),
        ],
        compiler_params=pltpu.CompilerParams(
            collective_id=0, has_side_effects=True, vmem_limit_bytes=48 * 1024 * 1024
        ),
    )(work_list, edge_kind.T, water_state, terrain)

def solution(mesh):
    placed = (
        P("groups", None, "tiles", None),
        P("groups", None, "tiles", None),
        P("groups"),
        P("groups", None),
    )
    return jax.shard_map(
        functools.partial(body, mesh.shape["tiles"]),
        mesh=mesh,
        in_specs=placed,
        out_specs=P("groups", None, "tiles", None),
        check_vma=False,
    )
```

```python
import functools

import jax
import jax.numpy as jnp
from jax import lax
from jax.experimental import pallas as pl
from jax.experimental.pallas import tpu as pltpu
from jax.sharding import PartitionSpec as P

TW = 16
ITERS = 4


GRAVITY = 9.81
DRY_DEPTH = 0.25
COURANT = 0.45


def roll_rows(x, shift):
    rows = x.shape[0]
    if rows % 8 == 0:
        return pltpu.roll(x, shift % rows, 0)
    cut = (rows - shift) % rows
    return jnp.concatenate([x[cut:], x[:cut]], axis=0)


def roll_lanes(x, shift):
    return pltpu.roll(x, shift % x.shape[1], 1)


def face(left, right):
    reach = jnp.maximum(left[1], right[1])
    mass = (left[0] + right[0]) - reach * (right[2] - left[2])
    first = (left[3] + right[3]) - reach * (right[0] - left[0])
    second = (left[4] + right[4]) - reach * (right[5] - left[5])
    return mass, first, second


def speeds(h, p, q):
    floored = jnp.maximum(h, DRY_DEPTH)
    root = lax.rsqrt(floored)
    inverse = root * root
    return p * inverse, q * inverse, (GRAVITY**0.5) * (floored * root)


def stepper(n, work, kinds, water, terrain, out, state, wv, tv, zs, rough, slope_x, slope_y, pace, derived,
            tend, rows_out, rows_in, z_out, z_in, ghost, ghost_z, landed, edge, edge_kinds, top_out, top_in,
            near, owner, local_sem, top_send, top_recv, row_send, row_recv, z_send, z_recv):
    count_tiles = water.shape[0]
    listed = state.shape[0]
    rows, width = state.shape[2], state.shape[3]
    half = width // 2
    me = lax.axis_index("tiles")
    at_first = me == 0
    at_final = me == n - 1

    barrier = pltpu.get_barrier_semaphore()
    for d in range(1, n):
        pl.semaphore_signal(
            barrier, inc=1, device_id={"tiles": lax.rem(me + d, n)}, device_id_type=pl.DeviceIdType.MESH
        )
    water_in = pltpu.make_async_copy(water, wv, local_sem.at[0])
    terrain_in = pltpu.make_async_copy(terrain, tv, local_sem.at[1])
    water_in.start()
    terrain_in.start()

    entries = [work[j] for j in range(listed)]

    def locate(s, carry):
        tile = work[s]
        chosen = jnp.minimum(tile, count_tiles - 1)
        active = tile < count_tiles
        found = [jnp.int32(0)] * 4
        sides = (chosen - TW, chosen + TW, chosen - 1, chosen + 1)
        for j in range(listed):
            found = [jnp.where(entries[j] == side, j, f) for side, f in zip(sides, found)]
        for e in range(4):
            near[e, s] = found[e]
            kind = jnp.where(active, kinds[e, chosen], 0)
            near[4 + e, s] = kind
            if e < 2:
                outer = jnp.where(at_first if e == 0 else at_final, kind, 1)
                edge_kinds[e, pl.ds(s, 1), :] = jnp.full((1, width), outer, jnp.int32)
        return carry

    lax.fori_loop(0, listed, locate, 0)

    def slots(one, unroll, carry=0):
        unroll = unroll if listed % unroll == 0 else 1

        def several(i, carry):
            for j in range(unroll):
                carry = one(i * unroll + j, carry)
            return carry

        return lax.fori_loop(0, listed // unroll, several, carry)

    row_at = lax.broadcasted_iota(jnp.int32, (rows, width), 0)
    lane_at = lax.broadcasted_iota(jnp.int32, (rows, half), 1)
    inner = row_at < rows - 1

    def settle(s, size, k, h, p, q, top):
        u, v, c = speeds(h, p, q)
        block = pl.ds(s, size)
        for i, x in enumerate((h, p, q)):
            state[block, i] = x
            for j in range(size):
                rows_out[k, 0, i, pl.ds(s + j, 1), :] = x[j, :1]
                rows_out[k, 1, i, pl.ds(s + j, 1), :] = x[j, rows - 1 :]
        for i, x in enumerate((u, v, c)):
            pace[block, i] = x
        fastest = jnp.maximum(jnp.abs(u), jnp.abs(v)) + c
        for j in range(size):
            top = jnp.maximum(top, jnp.where(work[s + j] < count_tiles, fastest[j], 0.0))
        return top

    def publish(k, top):
        part = jnp.max(top, axis=0, keepdims=True)
        top_out[k] = jnp.maximum(part[:, :half], part[:, half:])

    water_in.wait()
    terrain_in.wait()

    def gather(s, top):
        chosen = jnp.minimum(work[s], count_tiles - 1)
        z = tv[chosen, 0]
        zs[s] = z
        z_out[0, pl.ds(s, 1), :] = z[:1]
        z_out[1, pl.ds(s, 1), :] = z[rows - 1 :]
        return settle(s, 1, 0, *[wv[pl.ds(chosen, 1), i] for i in range(3)], top)

    publish(0, slots(gather, 2, jnp.zeros((rows, width), jnp.float32)))
    pl.semaphore_wait(barrier, n - 1)

    up = {"tiles": lax.rem(me + n - 1, n)}
    down = {"tiles": lax.rem(me + 1, n)}

    def remote(src, dst, send, recv, to):
        return pltpu.make_async_remote_copy(
            src_ref=src, dst_ref=dst, send_sem=send, recv_sem=recv, device_id=to,
            device_id_type=pl.DeviceIdType.MESH,
        )

    def top_copies(k):
        return [
            remote(top_out.at[k], top_in.at[k, d - 1], top_send.at[k, d - 1], top_recv.at[k, d - 1],
                   {"tiles": lax.rem(me + d, n)})
            for d in range(1, n)
        ]

    def row_copies(k):
        return [
            remote(rows_out.at[k, 0], rows_in.at[k, 1], row_send.at[k, 0], row_recv.at[k, 1], up),
            remote(rows_out.at[k, 1], rows_in.at[k, 0], row_send.at[k, 1], row_recv.at[k, 0], down),
        ]

    z_copies = [
        remote(z_out.at[0], z_in.at[1], z_send.at[0], z_recv.at[1], up),
        remote(z_out.at[1], z_in.at[0], z_send.at[1], z_recv.at[0], down),
    ]

    def prepare(s, carry):
        chosen = jnp.minimum(work[s], count_tiles - 1)
        z = zs[s]
        manning = tv[chosen, 1]
        rough[s] = (2.0 * GRAVITY) * manning * manning
        west_z = zs[near[2, s]][:, half:]
        east_z = zs[near[3, s]][:, :half]
        west_open = near[6, s] == 1
        east_open = near[7, s] == 1
        z_low, z_high = z[:, :half], z[:, half:]
        to_east = roll_lanes(z, -1)
        to_west = roll_lanes(z, 1)
        last = jnp.where(east_open, roll_lanes(east_z, -1), z_high)
        first = jnp.where(west_open, roll_lanes(west_z, 1), z_low)
        east = jnp.concatenate([to_east[:, :half], jnp.where(lane_at == half - 1, last, to_east[:, half:])], axis=1)
        west = jnp.concatenate([jnp.where(lane_at == 0, first, to_west[:, :half]), to_west[:, half:]], axis=1)
        slope_x[s] = GRAVITY * (east - west)
        south = jnp.where(inner, roll_rows(z, -1), 0.0)
        north = jnp.where(row_at == 0, 0.0, roll_rows(z, 1))
        slope_y[s] = GRAVITY * (south - north)
        share = -(-count_tiles // listed)
        for j in range(share):
            tile = jnp.minimum(s * share + j, count_tiles - 1)
            slot = jnp.int32(-1)
            for i in range(listed):
                slot = jnp.where(entries[i] == tile, i, slot)
            owner[tile] = slot
        return carry

    size = next(d for d in (4, 2, 1) if listed % d == 0)

    def derive(i, carry):
        block = pl.ds(i * size, size)
        h, p, q = state[block, 0], state[block, 1], state[block, 2]
        u, v, c = pace[block, 0], pace[block, 1], pace[block, 2]
        pressure = (0.5 * GRAVITY) * h * h
        derived[block, 0] = jnp.abs(u) + c
        derived[block, 1] = h + zs[block]
        derived[block, 2] = p * u + pressure
        derived[block, 3] = q * u
        derived[block, 4] = jnp.abs(v) + c
        derived[block, 5] = q * v + pressure
        floored = jnp.maximum(h, DRY_DEPTH)
        resist = jnp.exp2(jnp.log2(floored) * (-7.0 / 3.0))
        tend[block, 3] = rough[block] * jnp.sqrt(p * p + q * q) * resist
        return carry

    def along(s, lanes):
        return (state[s, 1, :, lanes], derived[s, 0, :, lanes], derived[s, 1, :, lanes],
                derived[s, 2, :, lanes], derived[s, 3, :, lanes], state[s, 2, :, lanes])

    low, high, whole = pl.ds(0, half), pl.ds(half, half), pl.ds(0, width)

    def balance(s, carry):
        own = along(s, whole)
        own_low = [x[:, :half] for x in own]
        own_high = [x[:, half:] for x in own]
        from_west = along(near[2, s], high)
        from_east = along(near[3, s], low)
        west_kind, east_kind = near[6, s], near[7, s]

        beyond = [
            roll_lanes(jnp.concatenate([jnp.where(lane_at == 0, g, a), b], axis=1), -1)
            for g, a, b in zip(from_east, own_low, own_high)
        ]
        flux = face(own, beyond)
        closed = 2.0 * own_high[1] * own_high[0]
        shut = (
            jnp.where(east_kind == 2, 2.0 * own_high[0], 0.0),
            2.0 * own_high[3] + jnp.where(east_kind == 0, closed, 0.0),
            jnp.where(east_kind == 2, 2.0 * own_high[4], 0.0),
        )
        rim = (lane_at == half - 1) & (east_kind != 1)
        flux = [
            jnp.concatenate([f[:, :half], jnp.where(rim, g, f[:, half:])], axis=1) for f, g in zip(flux, shut)
        ]
        entry = face([roll_lanes(x, 1) for x in from_west], own_low)
        closed = 2.0 * own_low[1] * own_low[0]
        shut = (
            jnp.where(west_kind == 2, 2.0 * own_low[0], 0.0),
            2.0 * own_low[3] - jnp.where(west_kind == 0, closed, 0.0),
            jnp.where(west_kind == 2, 2.0 * own_low[4], 0.0),
        )
        entry = [jnp.where(west_kind == 1, f, g) for f, g in zip(entry, shut)]
        change = []
        for f, g in zip(flux, entry):
            back = roll_lanes(f, 1)
            back = jnp.concatenate([jnp.where(lane_at == 0, g, back[:, :half]), back[:, half:]], axis=1)
            change.append(f - back)

        column = (own[5], derived[s, 4], own[2], derived[s, 5], own[4], own[0])
        flux = face(column, [roll_rows(x, -1) for x in column])
        flux = [jnp.where(inner, f, 0.0) for f in flux]
        across = [f - roll_rows(f, 1) for f in flux]
        h = state[s, 0]
        tend[s, 0] = change[0] + across[0]
        tend[s, 1] = change[1] + across[2] + h * slope_x[s]
        tend[s, 2] = change[2] + across[1] + h * slope_y[s]
        return carry

    def place_rows(side, source, target, channels):
        at_rim = at_first if side == 0 else at_final

        @pl.when(at_rim)
        def _():
            for i, index in enumerate(channels):
                landed[i] = source[index + (slice(None), slice(None))]

            def one(s, carry):
                nearby = near[side, s]
                for i, index in enumerate(channels):
                    target[(side,) + index + (pl.ds(s, 1), slice(None))] = landed[i, pl.ds(nearby, 1), :]
                return carry

            lax.fori_loop(0, listed, one, 0)

        @pl.when(jnp.logical_not(at_rim))
        def _():
            target[side] = source[...]

    def rim_cells(h, p, q, z):
        u, v, c = speeds(h, p, q)
        return (q, jnp.abs(v) + c, h + z, q * v + (0.5 * GRAVITY) * h * h, q * u, p)

    def rim(k, side):
        open_edge = edge_kinds[side] == 1
        wall = edge_kinds[side] == 0
        h, p, q, z = rows_out[k, side, 0], rows_out[k, side, 1], rows_out[k, side, 2], z_out[side]
        gh = jnp.where(open_edge, ghost[side, 0], h)
        gp = jnp.where(open_edge, ghost[side, 1], p)
        gq = jnp.where(open_edge, ghost[side, 2], jnp.where(wall, -q, q))
        gz = jnp.where(open_edge, ghost_z[side], z)
        mine, theirs = rim_cells(h, p, q, z), rim_cells(gh, gp, gq, gz)
        mass, first, second = face(theirs, mine) if side == 0 else face(mine, theirs)
        sign = -1.0 if side == 0 else 1.0
        edge[side, 0] = sign * mass
        edge[side, 1] = sign * second
        edge[side, 2] = sign * (first + GRAVITY * h * gz)

    def close_rows(s, carry):
        for i in range(3):
            tend[s, i, :1] += edge[0, i, pl.ds(s, 1), :]
            tend[s, i, rows - 1 :] += edge[1, i, pl.ds(s, 1), :]
        return carry

    def step(k, carry):
        tops, halos = top_copies(k), row_copies(k)
        for copy in tops:
            copy.start()
        for copy in halos:
            copy.start()

        @pl.when(k == 0)
        def _():
            for copy in z_copies:
                copy.start()
            slots(prepare, 2)

        lax.fori_loop(0, listed // size, derive, 0)
        slots(balance, 2)

        @pl.when(k == 0)
        def _():
            for copy in z_copies:
                copy.wait()
            for side in range(2):
                place_rows(side, z_in.at[side], ghost_z, [()])

        for copy in halos:
            copy.wait()
        for side in range(2):
            place_rows(side, rows_in.at[k, side], ghost, [(0,), (1,), (2,)])
            rim(k, side)
        slots(close_rows, 4)

        for copy in tops:
            copy.wait()
        top = jnp.maximum(jnp.max(top_in[k], axis=0), top_out[k])
        top = jnp.max(top, axis=1, keepdims=True)
        span = jnp.broadcast_to((COURANT / top) * 0.5, (rows, width))

        def update(i, top):
            block = pl.ds(i * size, size)
            h = state[block, 0] - span * tend[block, 0]
            root = lax.rsqrt(1.0 + span * tend[block, 3])
            damping = root * root
            p = (state[block, 1] - span * tend[block, 1]) * damping
            q = (state[block, 2] - span * tend[block, 2]) * damping
            return settle(i * size, size, k + 1, h, p, q, top)

        publish(k + 1, lax.fori_loop(0, listed // size, update, jnp.zeros((rows, width), jnp.float32)))
        return carry

    lax.fori_loop(0, ITERS, step, 0)

    def merge(t, carry):
        slot = owner[t]
        out[t] = jnp.where(slot >= 0, state[jnp.maximum(slot, 0)], wv[t])
        return carry

    lax.fori_loop(0, count_tiles, merge, 0)


def body(n, water_state, terrain, work_list, edge_kind):
    count_tiles, _, rows, width = water_state.shape
    listed = work_list.shape[0]
    smem = pl.BlockSpec(memory_space=pltpu.SMEM)
    anywhere = pl.BlockSpec(memory_space=pl.ANY)
    f32 = jnp.float32

    def vmem(*shape, dtype=f32):
        return pltpu.VMEM(shape, dtype)

    dma = pltpu.SemaphoreType.DMA
    return pl.pallas_call(
        functools.partial(stepper, n),
        out_shape=jax.ShapeDtypeStruct(water_state.shape, f32),
        in_specs=[smem, smem, anywhere, anywhere],
        out_specs=pl.BlockSpec(memory_space=pltpu.VMEM),
        scratch_shapes=[
            vmem(listed, 3, rows, width),
            vmem(count_tiles, 3, rows, width),
            vmem(count_tiles, 2, rows, width),
            vmem(listed, rows, width),
            vmem(listed, rows, width),
            vmem(listed, rows, width),
            vmem(listed, rows, width),
            vmem(listed, 3, rows, width),
            vmem(listed, 6, rows, width),
            vmem(listed, 4, rows, width),
            vmem(ITERS + 1, 2, 3, listed, width),
            vmem(ITERS, 2, 3, listed, width),
            vmem(2, listed, width),
            vmem(2, listed, width),
            vmem(2, 3, listed, width),
            vmem(2, listed, width),
            vmem(3, listed, width),
            vmem(2, 3, listed, width),
            vmem(2, listed, width, dtype=jnp.int32),
            vmem(ITERS + 1, 1, width // 2),
            vmem(ITERS, n - 1, 1, width // 2),
            pltpu.SMEM((8, listed), jnp.int32),
            pltpu.SMEM((count_tiles,), jnp.int32),
            dma((2,)),
            dma((ITERS, n - 1)),
            dma((ITERS, n - 1)),
            dma((ITERS, 2)),
            dma((ITERS, 2)),
            dma((2,)),
            dma((2,)),
        ],
        compiler_params=pltpu.CompilerParams(
            collective_id=0, has_side_effects=True, vmem_limit_bytes=48 * 1024 * 1024
        ),
    )(*[pltpu.with_memory_space_constraint(x, pltpu.HBM) for x in (work_list, edge_kind.T, water_state, terrain)])

def solution(mesh):
    placed = (
        P("groups", None, "tiles", None),
        P("groups", None, "tiles", None),
        P("groups"),
        P("groups", None),
    )
    return jax.shard_map(
        functools.partial(body, mesh.shape["tiles"]),
        mesh=mesh,
        in_specs=placed,
        out_specs=P("groups", None, "tiles", None),
        check_vma=False,
    )
```

```python
import functools

import jax
import jax.numpy as jnp
from jax import lax
from jax.experimental import pallas as pl
from jax.experimental.pallas import tpu as pltpu
from jax.sharding import PartitionSpec as P

TW = 16
ITERS = 4


GRAVITY = 9.81
DRY_DEPTH = 0.25
COURANT = 0.45


def roll_rows(x, shift):
    rows = x.shape[0]
    if rows % 8 == 0:
        return pltpu.roll(x, shift % rows, 0)
    cut = (rows - shift) % rows
    return jnp.concatenate([x[cut:], x[:cut]], axis=0)


def roll_lanes(x, shift):
    return pltpu.roll(x, shift % x.shape[1], 1)


def face(left, right):
    reach = jnp.maximum(left[1], right[1])
    mass = (left[0] + right[0]) - reach * (right[2] - left[2])
    first = (left[3] + right[3]) - reach * (right[0] - left[0])
    second = (left[4] + right[4]) - reach * (right[5] - left[5])
    return mass, first, second


def speeds(h, p, q):
    floored = jnp.maximum(h, DRY_DEPTH)
    root = lax.rsqrt(floored)
    inverse = root * root
    return p * inverse, q * inverse, (GRAVITY**0.5) * (floored * root)


def stepper(n, work, kinds, water, terrain, out, state, wv, tv, zs, rough, slope_x, slope_y, pace, derived,
            tend, rows_out, rows_in, z_out, z_in, ghost, ghost_z, landed, edge, edge_kinds, top_out, top_in,
            near, owner, local_sem, top_send, top_recv, row_send, row_recv, z_send, z_recv):
    count_tiles = water.shape[0]
    listed = state.shape[0]
    rows, width = state.shape[2], state.shape[3]
    half = width // 2
    me = lax.axis_index("tiles")
    at_first = me == 0
    at_final = me == n - 1

    others = [{"tiles": jnp.where(me + d < n, me + d, me + d - n)} for d in range(1, n)]
    down, up = others[0], others[-1]
    barrier = pltpu.get_barrier_semaphore()
    for other in others:
        pl.semaphore_signal(barrier, inc=1, device_id=other, device_id_type=pl.DeviceIdType.MESH)
    water_in = pltpu.make_async_copy(water, wv, local_sem.at[0])
    terrain_in = pltpu.make_async_copy(terrain, tv, local_sem.at[1])
    water_in.start()
    terrain_in.start()

    entries = [work[j] for j in range(listed)]

    def locate(s, carry):
        tile = work[s]
        chosen = jnp.minimum(tile, count_tiles - 1)
        active = tile < count_tiles
        found = [jnp.int32(0)] * 4
        sides = (chosen - TW, chosen + TW, chosen - 1, chosen + 1)
        for j in range(listed):
            found = [jnp.where(entries[j] == side, j, f) for side, f in zip(sides, found)]
        for e in range(4):
            near[e, s] = found[e]
            kind = jnp.where(active, kinds[e, chosen], 0)
            near[4 + e, s] = kind
            if e < 2:
                outer = jnp.where(at_first if e == 0 else at_final, kind, 1)
                edge_kinds[e, pl.ds(s, 1), :] = jnp.full((1, width), outer, jnp.int32)
        return carry

    lax.fori_loop(0, listed, locate, 0)

    def slots(one, unroll, carry=0):
        unroll = unroll if listed % unroll == 0 else 1

        def several(i, carry):
            for j in range(unroll):
                carry = one(i * unroll + j, carry)
            return carry

        return lax.fori_loop(0, listed // unroll, several, carry)

    row_at = lax.broadcasted_iota(jnp.int32, (rows, width), 0)
    lane_at = lax.broadcasted_iota(jnp.int32, (rows, half), 1)
    inner = row_at < rows - 1

    def settle(s, size, k, h, p, q, top):
        u, v, c = speeds(h, p, q)
        block = pl.ds(s, size)
        for i, x in enumerate((h, p, q)):
            state[block, i] = x
            for j in range(size):
                rows_out[k, 0, i, pl.ds(s + j, 1), :] = x[j, :1]
                rows_out[k, 1, i, pl.ds(s + j, 1), :] = x[j, rows - 1 :]
        for i, x in enumerate((u, v, c)):
            pace[block, i] = x
        fastest = jnp.maximum(jnp.abs(u), jnp.abs(v)) + c
        for j in range(size):
            top = jnp.maximum(top, jnp.where(work[s + j] < count_tiles, fastest[j], 0.0))
        return top

    def publish(k, top):
        part = jnp.max(top, axis=0, keepdims=True)
        top_out[k] = jnp.maximum(part[:, :half], part[:, half:])

    water_in.wait()

    def gather(s, top):
        chosen = jnp.minimum(work[s], count_tiles - 1)
        return settle(s, 1, 0, *[wv[pl.ds(chosen, 1), i] for i in range(3)], top)

    publish(0, slots(gather, 2, jnp.zeros((rows, width), jnp.float32)))
    pl.semaphore_wait(barrier, n - 1)

    def remote(src, dst, send, recv, to):
        return pltpu.make_async_remote_copy(
            src_ref=src, dst_ref=dst, send_sem=send, recv_sem=recv, device_id=to,
            device_id_type=pl.DeviceIdType.MESH,
        )

    def top_copies(k):
        return [
            remote(top_out.at[k], top_in.at[k, i], top_send.at[k], top_recv.at[k], other)
            for i, other in enumerate(others)
        ]

    def all_tops(k):
        return remote(top_in.at[k], top_in.at[k], top_send.at[k], top_recv.at[k], down)

    def row_copies(k):
        return [
            remote(rows_out.at[k, 0], rows_in.at[k, 1], row_send.at[k, 0], row_recv.at[k, 1], up),
            remote(rows_out.at[k, 1], rows_in.at[k, 0], row_send.at[k, 1], row_recv.at[k, 0], down),
        ]

    z_copies = [
        remote(z_out.at[0], z_in.at[1], z_send.at[0], z_recv.at[1], up),
        remote(z_out.at[1], z_in.at[0], z_send.at[1], z_recv.at[0], down),
    ]

    def ground(s, carry):
        z = tv[jnp.minimum(work[s], count_tiles - 1), 0]
        zs[s] = z
        z_out[0, pl.ds(s, 1), :] = z[:1]
        z_out[1, pl.ds(s, 1), :] = z[rows - 1 :]
        return carry

    def prepare(s, carry):
        chosen = jnp.minimum(work[s], count_tiles - 1)
        z = zs[s]
        manning = tv[chosen, 1]
        rough[s] = (2.0 * GRAVITY) * manning * manning
        west_z = zs[near[2, s]][:, half:]
        east_z = zs[near[3, s]][:, :half]
        west_open = near[6, s] == 1
        east_open = near[7, s] == 1
        z_low, z_high = z[:, :half], z[:, half:]
        to_east = roll_lanes(z, -1)
        to_west = roll_lanes(z, 1)
        last = jnp.where(east_open, roll_lanes(east_z, -1), z_high)
        first = jnp.where(west_open, roll_lanes(west_z, 1), z_low)
        east = jnp.concatenate([to_east[:, :half], jnp.where(lane_at == half - 1, last, to_east[:, half:])], axis=1)
        west = jnp.concatenate([jnp.where(lane_at == 0, first, to_west[:, :half]), to_west[:, half:]], axis=1)
        slope_x[s] = GRAVITY * (east - west)
        south = jnp.where(inner, roll_rows(z, -1), 0.0)
        north = jnp.where(row_at == 0, 0.0, roll_rows(z, 1))
        slope_y[s] = GRAVITY * (south - north)
        share = -(-count_tiles // listed)
        for j in range(share):
            tile = jnp.minimum(s * share + j, count_tiles - 1)
            slot = jnp.int32(-1)
            for i in range(listed):
                slot = jnp.where(entries[i] == tile, i, slot)
            owner[tile] = slot
        return carry

    size = next(d for d in (4, 2, 1) if listed % d == 0)

    def derive(i, carry):
        block = pl.ds(i * size, size)
        h, p, q = state[block, 0], state[block, 1], state[block, 2]
        u, v, c = pace[block, 0], pace[block, 1], pace[block, 2]
        pressure = (0.5 * GRAVITY) * h * h
        derived[block, 0] = jnp.abs(u) + c
        derived[block, 1] = h + zs[block]
        derived[block, 2] = p * u + pressure
        derived[block, 3] = q * u
        derived[block, 4] = jnp.abs(v) + c
        derived[block, 5] = q * v + pressure
        floored = jnp.maximum(h, DRY_DEPTH)
        resist = jnp.exp2(jnp.log2(floored) * (-7.0 / 3.0))
        tend[block, 3] = rough[block] * jnp.sqrt(p * p + q * q) * resist
        return carry

    def along(s, lanes):
        return (state[s, 1, :, lanes], derived[s, 0, :, lanes], derived[s, 1, :, lanes],
                derived[s, 2, :, lanes], derived[s, 3, :, lanes], state[s, 2, :, lanes])

    low, high, whole = pl.ds(0, half), pl.ds(half, half), pl.ds(0, width)

    def balance(s, carry):
        own = along(s, whole)
        own_low = [x[:, :half] for x in own]
        own_high = [x[:, half:] for x in own]
        from_west = along(near[2, s], high)
        from_east = along(near[3, s], low)
        west_kind, east_kind = near[6, s], near[7, s]

        beyond = [
            roll_lanes(jnp.concatenate([jnp.where(lane_at == 0, g, a), b], axis=1), -1)
            for g, a, b in zip(from_east, own_low, own_high)
        ]
        flux = face(own, beyond)
        closed = 2.0 * own_high[1] * own_high[0]
        shut = (
            jnp.where(east_kind == 2, 2.0 * own_high[0], 0.0),
            2.0 * own_high[3] + jnp.where(east_kind == 0, closed, 0.0),
            jnp.where(east_kind == 2, 2.0 * own_high[4], 0.0),
        )
        rim = (lane_at == half - 1) & (east_kind != 1)
        flux = [
            jnp.concatenate([f[:, :half], jnp.where(rim, g, f[:, half:])], axis=1) for f, g in zip(flux, shut)
        ]
        entry = face([roll_lanes(x, 1) for x in from_west], own_low)
        closed = 2.0 * own_low[1] * own_low[0]
        shut = (
            jnp.where(west_kind == 2, 2.0 * own_low[0], 0.0),
            2.0 * own_low[3] - jnp.where(west_kind == 0, closed, 0.0),
            jnp.where(west_kind == 2, 2.0 * own_low[4], 0.0),
        )
        entry = [jnp.where(west_kind == 1, f, g) for f, g in zip(entry, shut)]
        change = []
        for f, g in zip(flux, entry):
            back = roll_lanes(f, 1)
            back = jnp.concatenate([jnp.where(lane_at == 0, g, back[:, :half]), back[:, half:]], axis=1)
            change.append(f - back)

        column = (own[5], derived[s, 4], own[2], derived[s, 5], own[4], own[0])
        flux = face(column, [roll_rows(x, -1) for x in column])
        flux = [jnp.where(inner, f, 0.0) for f in flux]
        across = [f - roll_rows(f, 1) for f in flux]
        h = state[s, 0]
        tend[s, 0] = change[0] + across[0]
        tend[s, 1] = change[1] + across[2] + h * slope_x[s]
        tend[s, 2] = change[2] + across[1] + h * slope_y[s]
        return carry

    def place_rows(side, source, target, channels):
        at_rim = at_first if side == 0 else at_final

        @pl.when(at_rim)
        def _():
            for i, index in enumerate(channels):
                landed[i] = source[index + (slice(None), slice(None))]

            def one(s, carry):
                nearby = near[side, s]
                for i, index in enumerate(channels):
                    target[(side,) + index + (pl.ds(s, 1), slice(None))] = landed[i, pl.ds(nearby, 1), :]
                return carry

            lax.fori_loop(0, listed, one, 0)

        @pl.when(jnp.logical_not(at_rim))
        def _():
            target[side] = source[...]

    def rim_cells(h, p, q, z):
        u, v, c = speeds(h, p, q)
        return (q, jnp.abs(v) + c, h + z, q * v + (0.5 * GRAVITY) * h * h, q * u, p)

    def rim(k, side):
        open_edge = edge_kinds[side] == 1
        wall = edge_kinds[side] == 0
        h, p, q, z = rows_out[k, side, 0], rows_out[k, side, 1], rows_out[k, side, 2], z_out[side]
        gh = jnp.where(open_edge, ghost[side, 0], h)
        gp = jnp.where(open_edge, ghost[side, 1], p)
        gq = jnp.where(open_edge, ghost[side, 2], jnp.where(wall, -q, q))
        gz = jnp.where(open_edge, ghost_z[side], z)
        mine, theirs = rim_cells(h, p, q, z), rim_cells(gh, gp, gq, gz)
        mass, first, second = face(theirs, mine) if side == 0 else face(mine, theirs)
        sign = -1.0 if side == 0 else 1.0
        edge[side, 0] = sign * mass
        edge[side, 1] = sign * second
        edge[side, 2] = sign * (first + GRAVITY * h * gz)

    def close_rows(block, carry):
        ends = ((0, slice(0, 1)), (1, slice(rows - 1, rows)))
        at = [(block * size + j, i, side, row) for j in range(size) for i in range(3) for side, row in ends]
        closed = [tend[s, i, row] + edge[side, i, pl.ds(s, 1), :] for s, i, side, row in at]
        for (s, i, side, row), x in zip(at, closed):
            tend[s, i, row] = x
        return carry

    def step(k, carry):
        tops, halos = top_copies(k), row_copies(k)
        for copy in tops:
            copy.start()
        for copy in halos:
            copy.start()

        @pl.when(k == 0)
        def _():
            terrain_in.wait()
            slots(ground, 4)
            for copy in z_copies:
                copy.start()
            slots(prepare, 2)

        lax.fori_loop(0, listed // size, derive, 0)
        slots(balance, 2)

        @pl.when(k == 0)
        def _():
            for copy in z_copies:
                copy.wait_recv()
            for side in range(2):
                place_rows(side, z_in.at[side], ghost_z, [()])

        for copy in halos:
            copy.wait_recv()
        for side in range(2):
            place_rows(side, rows_in.at[k, side], ghost, [(0,), (1,), (2,)])
            rim(k, side)
        lax.fori_loop(0, listed // size, close_rows, 0)

        all_tops(k).wait_recv()
        top = jnp.maximum(jnp.max(top_in[k], axis=0), top_out[k])
        top = jnp.max(top, axis=1, keepdims=True)
        span = jnp.broadcast_to((COURANT / top) * 0.5, (rows, width))

        def update(i, top):
            block = pl.ds(i * size, size)
            h = state[block, 0] - span * tend[block, 0]
            root = lax.rsqrt(1.0 + span * tend[block, 3])
            damping = root * root
            p = (state[block, 1] - span * tend[block, 1]) * damping
            q = (state[block, 2] - span * tend[block, 2]) * damping
            return settle(i * size, size, k + 1, h, p, q, top)

        publish(k + 1, lax.fori_loop(0, listed // size, update, jnp.zeros((rows, width), jnp.float32)))
        return carry

    lax.fori_loop(0, ITERS, step, 0)

    spread = next(d for d in (4, 2, 1) if count_tiles % d == 0)

    def merge(i, carry):
        for j in range(spread):
            t = i * spread + j
            slot = owner[t]
            out[t] = jnp.where(slot >= 0, state[jnp.maximum(slot, 0)], wv[t])
        return carry

    lax.fori_loop(0, count_tiles // spread, merge, 0)

    for copy in z_copies:
        copy.wait_send()
    for k in range(ITERS):
        for copy in row_copies(k):
            copy.wait_send()
        all_tops(k).wait_send()


def body(n, water_state, terrain, work_list, edge_kind):
    count_tiles, _, rows, width = water_state.shape
    listed = work_list.shape[0]
    smem = pl.BlockSpec(memory_space=pltpu.SMEM)
    anywhere = pl.BlockSpec(memory_space=pl.ANY)
    f32 = jnp.float32

    def vmem(*shape, dtype=f32):
        return pltpu.VMEM(shape, dtype)

    dma = pltpu.SemaphoreType.DMA
    return pl.pallas_call(
        functools.partial(stepper, n),
        out_shape=jax.ShapeDtypeStruct(water_state.shape, f32),
        in_specs=[smem, smem, anywhere, anywhere],
        out_specs=pl.BlockSpec(memory_space=pltpu.VMEM),
        scratch_shapes=[
            vmem(listed, 3, rows, width),
            vmem(count_tiles, 3, rows, width),
            vmem(count_tiles, 2, rows, width),
            vmem(listed, rows, width),
            vmem(listed, rows, width),
            vmem(listed, rows, width),
            vmem(listed, rows, width),
            vmem(listed, 3, rows, width),
            vmem(listed, 6, rows, width),
            vmem(listed, 4, rows, width),
            vmem(ITERS + 1, 2, 3, listed, width),
            vmem(ITERS, 2, 3, listed, width),
            vmem(2, listed, width),
            vmem(2, listed, width),
            vmem(2, 3, listed, width),
            vmem(2, listed, width),
            vmem(3, listed, width),
            vmem(2, 3, listed, width),
            vmem(2, listed, width, dtype=jnp.int32),
            vmem(ITERS + 1, 1, width // 2),
            vmem(ITERS, n - 1, 1, width // 2),
            pltpu.SMEM((8, listed), jnp.int32),
            pltpu.SMEM((count_tiles,), jnp.int32),
            dma((2,)),
            dma((ITERS,)),
            dma((ITERS,)),
            dma((ITERS, 2)),
            dma((ITERS, 2)),
            dma((2,)),
            dma((2,)),
        ],
        compiler_params=pltpu.CompilerParams(
            collective_id=0, has_side_effects=True, vmem_limit_bytes=48 * 1024 * 1024
        ),
    )(*[pltpu.with_memory_space_constraint(x, pltpu.HBM) for x in (work_list, edge_kind.T, water_state, terrain)])

def solution(mesh):
    placed = (
        P("groups", None, "tiles", None),
        P("groups", None, "tiles", None),
        P("groups"),
        P("groups", None),
    )
    return jax.shard_map(
        functools.partial(body, mesh.shape["tiles"]),
        mesh=mesh,
        in_specs=placed,
        out_specs=P("groups", None, "tiles", None),
        check_vma=False,
    )
```

```python
import functools

import jax
import jax.numpy as jnp
from jax import lax
from jax.experimental import pallas as pl
from jax.experimental.pallas import tpu as pltpu
from jax.sharding import PartitionSpec as P

TW = 16
ITERS = 4


GRAVITY = 9.81
DRY_DEPTH = 0.25
COURANT = 0.45


def roll_rows(x, shift):
    rows = x.shape[0]
    if rows % 8 == 0:
        return pltpu.roll(x, shift % rows, 0)
    cut = (rows - shift) % rows
    return jnp.concatenate([x[cut:], x[:cut]], axis=0)


def roll_lanes(x, shift):
    return pltpu.roll(x, shift % x.shape[1], 1)


def face(left, right):
    reach = jnp.maximum(left[1], right[1])
    mass = (left[0] + right[0]) - reach * (right[2] - left[2])
    first = (left[3] + right[3]) - reach * (right[0] - left[0])
    second = (left[4] + right[4]) - reach * (right[5] - left[5])
    return mass, first, second


def speeds(h, p, q):
    floored = jnp.maximum(h, DRY_DEPTH)
    root = lax.rsqrt(floored)
    inverse = root * root
    return p * inverse, q * inverse, (GRAVITY**0.5) * (floored * root)


def stepper(n, work, kinds, water, terrain, out, state, wv, tv, zs, rough, slope_x, slope_y, derived,
            tend, rows_out, rows_in, z_out, z_in, ghost, ghost_z, landed, edge, edge_kinds, top_out, top_in,
            near, owner, local_sem, top_send, top_recv, row_send, row_recv, z_send, z_recv):
    count_tiles = water.shape[0]
    listed = state.shape[0]
    rows, width = state.shape[2], state.shape[3]
    half = width // 2
    me = lax.axis_index("tiles")
    at_first = me == 0
    at_final = me == n - 1

    others = [{"tiles": jnp.where(me + d < n, me + d, me + d - n)} for d in range(1, n)]
    down, up = others[0], others[-1]
    barrier = pltpu.get_barrier_semaphore()
    for other in others:
        pl.semaphore_signal(barrier, inc=1, device_id=other, device_id_type=pl.DeviceIdType.MESH)
    water_in = pltpu.make_async_copy(water, wv, local_sem.at[0])
    terrain_in = pltpu.make_async_copy(terrain, tv, local_sem.at[1])
    water_in.start()
    terrain_in.start()

    entries = [work[j] for j in range(listed)]

    def locate(s, carry):
        tile = work[s]
        chosen = jnp.minimum(tile, count_tiles - 1)
        active = tile < count_tiles
        found = [jnp.int32(0)] * 4
        sides = (chosen - TW, chosen + TW, chosen - 1, chosen + 1)
        for j in range(listed):
            found = [jnp.where(entries[j] == side, j, f) for side, f in zip(sides, found)]
        for e in range(4):
            near[e, s] = found[e]
            kind = jnp.where(active, kinds[e, chosen], 0)
            near[4 + e, s] = kind
            if e < 2:
                outer = jnp.where(at_first if e == 0 else at_final, kind, 1)
                edge_kinds[e, pl.ds(s, 1), :] = jnp.full((1, width), outer, jnp.int32)
        return carry

    lax.fori_loop(0, listed, locate, 0)

    def slots(one, unroll, carry=0):
        unroll = unroll if listed % unroll == 0 else 1

        def several(i, carry):
            for j in range(unroll):
                carry = one(i * unroll + j, carry)
            return carry

        return lax.fori_loop(0, listed // unroll, several, carry)

    row_at = lax.broadcasted_iota(jnp.int32, (rows, width), 0)
    lane_at = lax.broadcasted_iota(jnp.int32, (rows, half), 1)
    inner = row_at < rows - 1

    def settle(s, size, h, p, q, top):
        u, v, c = speeds(h, p, q)
        block = pl.ds(s, size)
        for i, x in enumerate((h, p, q)):
            state[block, i] = x
        fastest = jnp.maximum(jnp.abs(u), jnp.abs(v)) + c
        for j in range(size):
            top = jnp.maximum(top, jnp.where(work[s + j] < count_tiles, fastest[j], 0.0))
        return top

    def publish(k, top):
        part = jnp.max(top, axis=0, keepdims=True)
        top_out[k] = jnp.maximum(part[:, :half], part[:, half:])

    water_in.wait()

    def gather(s, top):
        chosen = jnp.minimum(work[s], count_tiles - 1)
        return settle(s, 1, *[wv[pl.ds(chosen, 1), i] for i in range(3)], top)

    publish(0, slots(gather, 2, jnp.zeros((rows, width), jnp.float32)))
    pl.semaphore_wait(barrier, n - 1)

    def remote(src, dst, send, recv, to):
        return pltpu.make_async_remote_copy(
            src_ref=src, dst_ref=dst, send_sem=send, recv_sem=recv, device_id=to,
            device_id_type=pl.DeviceIdType.MESH,
        )

    def top_copies(k):
        return [
            remote(top_out.at[k], top_in.at[k, i], top_send.at[k], top_recv.at[k], other)
            for i, other in enumerate(others)
        ]

    def all_tops(k):
        return remote(top_in.at[k], top_in.at[k], top_send.at[k], top_recv.at[k], down)

    def row_copies(k):
        return [
            remote(rows_out.at[k, 0], rows_in.at[k, 1], row_send.at[k, 0], row_recv.at[k, 1], up),
            remote(rows_out.at[k, 1], rows_in.at[k, 0], row_send.at[k, 1], row_recv.at[k, 0], down),
        ]

    z_copies = [
        remote(z_out.at[0], z_in.at[1], z_send.at[0], z_recv.at[1], up),
        remote(z_out.at[1], z_in.at[0], z_send.at[1], z_recv.at[0], down),
    ]

    def ground(s, carry):
        z = tv[jnp.minimum(work[s], count_tiles - 1), 0]
        zs[s] = z
        z_out[0, pl.ds(s, 1), :] = z[:1]
        z_out[1, pl.ds(s, 1), :] = z[rows - 1 :]
        return carry

    def prepare(s, carry):
        chosen = jnp.minimum(work[s], count_tiles - 1)
        z = zs[s]
        manning = tv[chosen, 1]
        rough[s] = (2.0 * GRAVITY) * manning * manning
        west_z = zs[near[2, s]][:, half:]
        east_z = zs[near[3, s]][:, :half]
        west_open = near[6, s] == 1
        east_open = near[7, s] == 1
        z_low, z_high = z[:, :half], z[:, half:]
        to_east = roll_lanes(z, -1)
        to_west = roll_lanes(z, 1)
        last = jnp.where(east_open, roll_lanes(east_z, -1), z_high)
        first = jnp.where(west_open, roll_lanes(west_z, 1), z_low)
        east = jnp.concatenate([to_east[:, :half], jnp.where(lane_at == half - 1, last, to_east[:, half:])], axis=1)
        west = jnp.concatenate([jnp.where(lane_at == 0, first, to_west[:, :half]), to_west[:, half:]], axis=1)
        slope_x[s] = GRAVITY * (east - west)
        south = jnp.where(inner, roll_rows(z, -1), 0.0)
        north = jnp.where(row_at == 0, 0.0, roll_rows(z, 1))
        slope_y[s] = GRAVITY * (south - north)
        share = -(-count_tiles // listed)
        for j in range(share):
            tile = jnp.minimum(s * share + j, count_tiles - 1)
            slot = jnp.int32(-1)
            for i in range(listed):
                slot = jnp.where(entries[i] == tile, i, slot)
            owner[tile] = slot
        return carry

    size = next(d for d in (4, 2, 1) if listed % d == 0)

    def derive(i, carry):
        block = pl.ds(i * size, size)
        h, p, q = state[block, 0], state[block, 1], state[block, 2]
        u, v, c = speeds(h, p, q)
        pressure = (0.5 * GRAVITY) * h * h
        derived[block, 0] = jnp.abs(u) + c
        derived[block, 1] = h + zs[block]
        derived[block, 2] = p * u + pressure
        derived[block, 3] = q * u
        derived[block, 4] = jnp.abs(v) + c
        derived[block, 5] = q * v + pressure
        floored = jnp.maximum(h, DRY_DEPTH)
        resist = jnp.exp(jnp.log(floored) * (-7.0 / 3.0))
        tend[block, 3] = rough[block] * jnp.sqrt(p * p + q * q) * resist
        return carry

    def along(s, lanes):
        return (state[s, 1, :, lanes], derived[s, 0, :, lanes], derived[s, 1, :, lanes],
                derived[s, 2, :, lanes], derived[s, 3, :, lanes], state[s, 2, :, lanes])

    low, high, whole = pl.ds(0, half), pl.ds(half, half), pl.ds(0, width)

    def balance(s, carry):
        own = along(s, whole)
        own_low = [x[:, :half] for x in own]
        own_high = [x[:, half:] for x in own]
        from_west = along(near[2, s], high)
        from_east = along(near[3, s], low)
        west_kind, east_kind = near[6, s], near[7, s]

        beyond = [
            roll_lanes(jnp.concatenate([jnp.where(lane_at == 0, g, a), b], axis=1), -1)
            for g, a, b in zip(from_east, own_low, own_high)
        ]
        flux = face(own, beyond)
        closed = 2.0 * own_high[1] * own_high[0]
        shut = (
            jnp.where(east_kind == 2, 2.0 * own_high[0], 0.0),
            2.0 * own_high[3] + jnp.where(east_kind == 0, closed, 0.0),
            jnp.where(east_kind == 2, 2.0 * own_high[4], 0.0),
        )
        rim = (lane_at == half - 1) & (east_kind != 1)
        flux = [
            jnp.concatenate([f[:, :half], jnp.where(rim, g, f[:, half:])], axis=1) for f, g in zip(flux, shut)
        ]
        entry = face([roll_lanes(x, 1) for x in from_west], own_low)
        closed = 2.0 * own_low[1] * own_low[0]
        shut = (
            jnp.where(west_kind == 2, 2.0 * own_low[0], 0.0),
            2.0 * own_low[3] - jnp.where(west_kind == 0, closed, 0.0),
            jnp.where(west_kind == 2, 2.0 * own_low[4], 0.0),
        )
        entry = [jnp.where(west_kind == 1, f, g) for f, g in zip(entry, shut)]
        change = []
        for f, g in zip(flux, entry):
            back = roll_lanes(f, 1)
            back = jnp.concatenate([jnp.where(lane_at == 0, g, back[:, :half]), back[:, half:]], axis=1)
            change.append(f - back)

        column = (own[5], derived[s, 4], own[2], derived[s, 5], own[4], own[0])
        flux = face(column, [roll_rows(x, -1) for x in column])
        flux = [jnp.where(inner, f, 0.0) for f in flux]
        across = [f - roll_rows(f, 1) for f in flux]
        h = state[s, 0]
        tend[s, 0] = change[0] + across[0]
        tend[s, 1] = change[1] + across[2] + h * slope_x[s]
        tend[s, 2] = change[2] + across[1] + h * slope_y[s]
        return carry

    def place_rows(side, source, target, channels):
        at_rim = at_first if side == 0 else at_final

        @pl.when(at_rim)
        def _():
            for i, index in enumerate(channels):
                landed[i] = source[index + (slice(None), slice(None))]

            def one(s, carry):
                nearby = near[side, s]
                for i, index in enumerate(channels):
                    target[(side,) + index + (pl.ds(s, 1), slice(None))] = landed[i, pl.ds(nearby, 1), :]
                return carry

            slots(one, 4)

        @pl.when(jnp.logical_not(at_rim))
        def _():
            target[side] = source[...]

    def rim_cells(h, p, q, z):
        u, v, c = speeds(h, p, q)
        return (q, jnp.abs(v) + c, h + z, q * v + (0.5 * GRAVITY) * h * h, q * u, p)

    def rim(k, side):
        open_edge = edge_kinds[side] == 1
        wall = edge_kinds[side] == 0
        h, p, q, z = rows_out[k, side, 0], rows_out[k, side, 1], rows_out[k, side, 2], z_out[side]
        gh = jnp.where(open_edge, ghost[side, 0], h)
        gp = jnp.where(open_edge, ghost[side, 1], p)
        gq = jnp.where(open_edge, ghost[side, 2], jnp.where(wall, -q, q))
        gz = jnp.where(open_edge, ghost_z[side], z)
        mine, theirs = rim_cells(h, p, q, z), rim_cells(gh, gp, gq, gz)
        mass, first, second = face(theirs, mine) if side == 0 else face(mine, theirs)
        sign = -1.0 if side == 0 else 1.0
        edge[side, 0] = sign * mass
        edge[side, 1] = sign * second
        edge[side, 2] = sign * (first + GRAVITY * h * gz)

    ends = ((0, slice(0, 1)), (1, slice(rows - 1, rows)))

    def pack(k, block, carry):
        at = [(block * size + j, i, side, row) for j in range(size) for i in range(3) for side, row in ends]
        kept = [state[s, i, row] for s, i, side, row in at]
        for (s, i, side, row), x in zip(at, kept):
            rows_out[k, side, i, pl.ds(s, 1), :] = x
        return carry

    def close_rows(block, carry):
        at = [(block * size + j, i, side, row) for j in range(size) for i in range(3) for side, row in ends]
        closed = [tend[s, i, row] + edge[side, i, pl.ds(s, 1), :] for s, i, side, row in at]
        for (s, i, side, row), x in zip(at, closed):
            tend[s, i, row] = x
        return carry

    def step(k, carry):
        tops, halos = top_copies(k), row_copies(k)
        for copy in tops:
            copy.start()
        lax.fori_loop(0, listed // size, functools.partial(pack, k), 0)
        for copy in halos:
            copy.start()

        @pl.when(k == 0)
        def _():
            terrain_in.wait()
            slots(ground, 4)
            for copy in z_copies:
                copy.start()
            slots(prepare, 2)

        lax.fori_loop(0, listed // size, derive, 0)
        slots(balance, 2)

        @pl.when(k == 0)
        def _():
            for copy in z_copies:
                copy.wait_recv()
            for side in range(2):
                place_rows(side, z_in.at[side], ghost_z, [()])

        for copy in halos:
            copy.wait_recv()
        for side in range(2):
            place_rows(side, rows_in.at[k, side], ghost, [(0,), (1,), (2,)])
            rim(k, side)
        lax.fori_loop(0, listed // size, close_rows, 0)

        all_tops(k).wait_recv()
        top = jnp.maximum(jnp.max(top_in[k], axis=0), top_out[k])
        top = jnp.max(top, axis=1, keepdims=True)
        span = jnp.broadcast_to((COURANT / top) * 0.5, (rows, width))

        def update(i, top):
            block = pl.ds(i * size, size)
            h = state[block, 0] - span * tend[block, 0]
            root = lax.rsqrt(1.0 + span * tend[block, 3])
            damping = root * root
            p = (state[block, 1] - span * tend[block, 1]) * damping
            q = (state[block, 2] - span * tend[block, 2]) * damping
            return settle(i * size, size, h, p, q, top)

        publish(k + 1, lax.fori_loop(0, listed // size, update, jnp.zeros((rows, width), jnp.float32)))
        return carry

    lax.fori_loop(0, ITERS, step, 0)

    spread = next(d for d in (4, 2, 1) if count_tiles % d == 0)

    def merge(i, carry):
        for j in range(spread):
            t = i * spread + j
            slot = owner[t]
            out[t] = jnp.where(slot >= 0, state[jnp.maximum(slot, 0)], wv[t])
        return carry

    lax.fori_loop(0, count_tiles // spread, merge, 0)

    for copy in z_copies:
        copy.wait_send()
    for k in range(ITERS):
        for copy in row_copies(k):
            copy.wait_send()
        all_tops(k).wait_send()


def body(n, water_state, terrain, work_list, edge_kind):
    count_tiles, _, rows, width = water_state.shape
    listed = work_list.shape[0]
    smem = pl.BlockSpec(memory_space=pltpu.SMEM)
    anywhere = pl.BlockSpec(memory_space=pl.ANY)
    f32 = jnp.float32

    def vmem(*shape, dtype=f32):
        return pltpu.VMEM(shape, dtype)

    dma = pltpu.SemaphoreType.DMA
    return pl.pallas_call(
        functools.partial(stepper, n),
        out_shape=jax.ShapeDtypeStruct(water_state.shape, f32),
        in_specs=[smem, smem, anywhere, anywhere],
        out_specs=pl.BlockSpec(memory_space=pltpu.VMEM),
        scratch_shapes=[
            vmem(listed, 3, rows, width),
            vmem(count_tiles, 3, rows, width),
            vmem(count_tiles, 2, rows, width),
            vmem(listed, rows, width),
            vmem(listed, rows, width),
            vmem(listed, rows, width),
            vmem(listed, rows, width),
            vmem(listed, 6, rows, width),
            vmem(listed, 4, rows, width),
            vmem(ITERS, 2, 3, listed, width),
            vmem(ITERS, 2, 3, listed, width),
            vmem(2, listed, width),
            vmem(2, listed, width),
            vmem(2, 3, listed, width),
            vmem(2, listed, width),
            vmem(3, listed, width),
            vmem(2, 3, listed, width),
            vmem(2, listed, width, dtype=jnp.int32),
            vmem(ITERS + 1, 1, width // 2),
            vmem(ITERS, n - 1, 1, width // 2),
            pltpu.SMEM((8, listed), jnp.int32),
            pltpu.SMEM((count_tiles,), jnp.int32),
            dma((2,)),
            dma((ITERS,)),
            dma((ITERS,)),
            dma((ITERS, 2)),
            dma((ITERS, 2)),
            dma((2,)),
            dma((2,)),
        ],
        compiler_params=pltpu.CompilerParams(
            collective_id=0, has_side_effects=True, vmem_limit_bytes=48 * 1024 * 1024
        ),
    )(*[pltpu.with_memory_space_constraint(x, pltpu.HBM) for x in (work_list, edge_kind.T, water_state, terrain)])

def solution(mesh):
    placed = (
        P("groups", None, "tiles", None),
        P("groups", None, "tiles", None),
        P("groups"),
        P("groups", None),
    )
    return jax.shard_map(
        functools.partial(body, mesh.shape["tiles"]),
        mesh=mesh,
        in_specs=placed,
        out_specs=P("groups", None, "tiles", None),
        check_vma=False,
    )
```

```python
import functools

import jax
import jax.numpy as jnp
from jax import lax
from jax.experimental import pallas as pl
from jax.experimental.pallas import tpu as pltpu
from jax.sharding import PartitionSpec as P

TW = 16
ITERS = 4


GRAVITY = 9.81
DRY_DEPTH = 0.25
COURANT = 0.45


def roll_rows(x, shift):
    rows = x.shape[0]
    if rows % 8 == 0:
        return pltpu.roll(x, shift % rows, 0)
    cut = (rows - shift) % rows
    return jnp.concatenate([x[cut:], x[:cut]], axis=0)


def roll_lanes(x, shift):
    return pltpu.roll(x, shift % x.shape[1], 1)


def face(left, right):
    reach = jnp.maximum(left[1], right[1])
    mass = (left[0] + right[0]) - reach * (right[2] - left[2])
    first = (left[3] + right[3]) - reach * (right[0] - left[0])
    second = (left[4] + right[4]) - reach * (right[5] - left[5])
    return mass, first, second


def speeds(h, p, q):
    floored = jnp.maximum(h, DRY_DEPTH)
    root = lax.rsqrt(floored)
    inverse = root * root
    return p * inverse, q * inverse, (GRAVITY**0.5) * (floored * root)


def stepper(n, parts, work, kinds, water, terrain, out, state, wv, tv, zs, rough, slope_x, slope_y, derived,
            tend, rows_out, rows_in, z_out, z_in, ghost, ghost_z, landed, edge, edge_kinds, top_out, top_in,
            near, owner, local_sem, top_send, top_recv, row_send, row_recv, z_send, z_recv):
    count_tiles = water.shape[0]
    listed = state.shape[0]
    rows, width = state.shape[2], state.shape[3]
    half = width // 2
    me = lax.axis_index("tiles")
    at_first = me == 0
    at_final = me == n - 1

    chunk = listed // parts
    others = [{"tiles": jnp.where(me + d < n, me + d, me + d - n)} for d in range(1, n)]
    down, up = others[0], others[-1]
    barrier = pltpu.get_barrier_semaphore()
    for other in others:
        pl.semaphore_signal(barrier, inc=1, device_id=other, device_id_type=pl.DeviceIdType.MESH)
    water_in = pltpu.make_async_copy(water, wv, local_sem.at[0])
    terrain_in = pltpu.make_async_copy(terrain, tv, local_sem.at[1])
    water_in.start()
    terrain_in.start()

    entries = [work[j] for j in range(listed)]

    def locate(s, carry):
        tile = work[s]
        chosen = jnp.minimum(tile, count_tiles - 1)
        active = tile < count_tiles
        found = [jnp.int32(0)] * 4
        sides = (chosen - TW, chosen + TW, chosen - 1, chosen + 1)
        for j in range(listed):
            found = [jnp.where(entries[j] == side, j, f) for side, f in zip(sides, found)]
        for e in range(4):
            near[e, s] = found[e]
            kind = jnp.where(active, kinds[e, chosen], 0)
            near[4 + e, s] = kind
            if e < 2:
                outer = jnp.where(at_first if e == 0 else at_final, kind, 1)
                edge_kinds[e, pl.ds(s, 1), :] = jnp.full((1, width), outer, jnp.int32)
        return carry

    lax.fori_loop(0, listed, locate, 0)

    def slots(one, unroll, carry=0):
        unroll = unroll if listed % unroll == 0 else 1

        def several(i, carry):
            for j in range(unroll):
                carry = one(i * unroll + j, carry)
            return carry

        return lax.fori_loop(0, listed // unroll, several, carry)

    row_at = lax.broadcasted_iota(jnp.int32, (rows, width), 0)
    lane_at = lax.broadcasted_iota(jnp.int32, (rows, half), 1)
    inner = row_at < rows - 1

    def settle(s, size, h, p, q, top):
        u, v, c = speeds(h, p, q)
        block = pl.ds(s, size)
        for i, x in enumerate((h, p, q)):
            state[block, i] = x
        fastest = jnp.maximum(jnp.abs(u), jnp.abs(v)) + c
        for j in range(size):
            top = jnp.maximum(top, jnp.where(work[s + j] < count_tiles, fastest[j], 0.0))
        return top

    def publish(k, top):
        part = jnp.max(top, axis=0, keepdims=True)
        top_out[k] = jnp.maximum(part[:, :half], part[:, half:])

    water_in.wait()

    def gather(s, top):
        chosen = jnp.minimum(work[s], count_tiles - 1)
        return settle(s, 1, *[wv[pl.ds(chosen, 1), i] for i in range(3)], top)

    publish(0, slots(gather, 2, jnp.zeros((rows, width), jnp.float32)))
    pl.semaphore_wait(barrier, n - 1)

    def remote(src, dst, send, recv, to):
        return pltpu.make_async_remote_copy(
            src_ref=src, dst_ref=dst, send_sem=send, recv_sem=recv, device_id=to,
            device_id_type=pl.DeviceIdType.MESH,
        )

    def top_copies(k):
        return [
            remote(top_out.at[k], top_in.at[k, i], top_send.at[k], top_recv.at[k], other)
            for i, other in enumerate(others)
        ]

    def all_tops(k):
        return remote(top_in.at[k], top_in.at[k], top_send.at[k], top_recv.at[k], down)

    def row_copies(k, part):
        block = pl.ds(part * chunk, chunk)
        return [
            remote(rows_out.at[k, 0, :, block], rows_in.at[k, 1, :, block],
                   row_send.at[k, 0, part], row_recv.at[k, 1, part], up),
            remote(rows_out.at[k, 1, :, block], rows_in.at[k, 0, :, block],
                   row_send.at[k, 1, part], row_recv.at[k, 0, part], down),
        ]

    z_copies = [
        remote(z_out.at[0], z_in.at[1], z_send.at[0], z_recv.at[1], up),
        remote(z_out.at[1], z_in.at[0], z_send.at[1], z_recv.at[0], down),
    ]

    def ground(s, carry):
        z = tv[jnp.minimum(work[s], count_tiles - 1), 0]
        zs[s] = z
        z_out[0, pl.ds(s, 1), :] = z[:1]
        z_out[1, pl.ds(s, 1), :] = z[rows - 1 :]
        return carry

    def prepare(s, carry):
        chosen = jnp.minimum(work[s], count_tiles - 1)
        z = zs[s]
        manning = tv[chosen, 1]
        rough[s] = (2.0 * GRAVITY) * manning * manning
        west_z = zs[near[2, s]][:, half:]
        east_z = zs[near[3, s]][:, :half]
        west_open = near[6, s] == 1
        east_open = near[7, s] == 1
        z_low, z_high = z[:, :half], z[:, half:]
        to_east = roll_lanes(z, -1)
        to_west = roll_lanes(z, 1)
        last = jnp.where(east_open, roll_lanes(east_z, -1), z_high)
        first = jnp.where(west_open, roll_lanes(west_z, 1), z_low)
        east = jnp.concatenate([to_east[:, :half], jnp.where(lane_at == half - 1, last, to_east[:, half:])], axis=1)
        west = jnp.concatenate([jnp.where(lane_at == 0, first, to_west[:, :half]), to_west[:, half:]], axis=1)
        slope_x[s] = GRAVITY * (east - west)
        south = jnp.where(inner, roll_rows(z, -1), 0.0)
        north = jnp.where(row_at == 0, 0.0, roll_rows(z, 1))
        slope_y[s] = GRAVITY * (south - north)
        share = -(-count_tiles // listed)
        for j in range(share):
            tile = jnp.minimum(s * share + j, count_tiles - 1)
            slot = jnp.int32(-1)
            for i in range(listed):
                slot = jnp.where(entries[i] == tile, i, slot)
            owner[tile] = slot
        return carry

    size = next(d for d in (4, 2, 1) if chunk % d == 0)

    def derive(i, carry):
        block = pl.ds(i * size, size)
        h, p, q = state[block, 0], state[block, 1], state[block, 2]
        u, v, c = speeds(h, p, q)
        pressure = (0.5 * GRAVITY) * h * h
        derived[block, 0] = jnp.abs(u) + c
        derived[block, 1] = h + zs[block]
        derived[block, 2] = p * u + pressure
        derived[block, 3] = q * u
        derived[block, 4] = jnp.abs(v) + c
        derived[block, 5] = q * v + pressure
        floored = jnp.maximum(h, DRY_DEPTH)
        resist = jnp.exp(jnp.log(floored) * (-7.0 / 3.0))
        tend[block, 3] = rough[block] * jnp.sqrt(p * p + q * q) * resist
        return carry

    def along(s, lanes):
        return (state[s, 1, :, lanes], derived[s, 0, :, lanes], derived[s, 1, :, lanes],
                derived[s, 2, :, lanes], derived[s, 3, :, lanes], state[s, 2, :, lanes])

    low, high, whole = pl.ds(0, half), pl.ds(half, half), pl.ds(0, width)

    def balance(s, carry):
        own = along(s, whole)
        own_low = [x[:, :half] for x in own]
        own_high = [x[:, half:] for x in own]
        from_west = along(near[2, s], high)
        from_east = along(near[3, s], low)
        west_kind, east_kind = near[6, s], near[7, s]

        beyond = [
            roll_lanes(jnp.concatenate([jnp.where(lane_at == 0, g, a), b], axis=1), -1)
            for g, a, b in zip(from_east, own_low, own_high)
        ]
        flux = face(own, beyond)
        closed = 2.0 * own_high[1] * own_high[0]
        shut = (
            jnp.where(east_kind == 2, 2.0 * own_high[0], 0.0),
            2.0 * own_high[3] + jnp.where(east_kind == 0, closed, 0.0),
            jnp.where(east_kind == 2, 2.0 * own_high[4], 0.0),
        )
        rim = (lane_at == half - 1) & (east_kind != 1)
        flux = [
            jnp.concatenate([f[:, :half], jnp.where(rim, g, f[:, half:])], axis=1) for f, g in zip(flux, shut)
        ]
        entry = face([roll_lanes(x, 1) for x in from_west], own_low)
        closed = 2.0 * own_low[1] * own_low[0]
        shut = (
            jnp.where(west_kind == 2, 2.0 * own_low[0], 0.0),
            2.0 * own_low[3] - jnp.where(west_kind == 0, closed, 0.0),
            jnp.where(west_kind == 2, 2.0 * own_low[4], 0.0),
        )
        entry = [jnp.where(west_kind == 1, f, g) for f, g in zip(entry, shut)]
        change = []
        for f, g in zip(flux, entry):
            back = roll_lanes(f, 1)
            back = jnp.concatenate([jnp.where(lane_at == 0, g, back[:, :half]), back[:, half:]], axis=1)
            change.append(f - back)

        column = (own[5], derived[s, 4], own[2], derived[s, 5], own[4], own[0])
        flux = face(column, [roll_rows(x, -1) for x in column])
        flux = [jnp.where(inner, f, 0.0) for f in flux]
        across = [f - roll_rows(f, 1) for f in flux]
        h = state[s, 0]
        tend[s, 0] = change[0] + across[0]
        tend[s, 1] = change[1] + across[2] + h * slope_x[s]
        tend[s, 2] = change[2] + across[1] + h * slope_y[s]
        return carry

    def place_rows(side, source, target, channels):
        at_rim = at_first if side == 0 else at_final

        @pl.when(at_rim)
        def _():
            for i, index in enumerate(channels):
                landed[i] = source[index + (slice(None), slice(None))]

            def one(s, carry):
                nearby = near[side, s]
                for i, index in enumerate(channels):
                    target[(side,) + index + (pl.ds(s, 1), slice(None))] = landed[i, pl.ds(nearby, 1), :]
                return carry

            slots(one, 4)

        @pl.when(jnp.logical_not(at_rim))
        def _():
            target[side] = source[...]

    def rim_cells(h, p, q, z):
        u, v, c = speeds(h, p, q)
        return (q, jnp.abs(v) + c, h + z, q * v + (0.5 * GRAVITY) * h * h, q * u, p)

    def rim(k, side):
        open_edge = edge_kinds[side] == 1
        wall = edge_kinds[side] == 0
        h, p, q, z = rows_out[k, side, 0], rows_out[k, side, 1], rows_out[k, side, 2], z_out[side]
        gh = jnp.where(open_edge, ghost[side, 0], h)
        gp = jnp.where(open_edge, ghost[side, 1], p)
        gq = jnp.where(open_edge, ghost[side, 2], jnp.where(wall, -q, q))
        gz = jnp.where(open_edge, ghost_z[side], z)
        mine, theirs = rim_cells(h, p, q, z), rim_cells(gh, gp, gq, gz)
        mass, first, second = face(theirs, mine) if side == 0 else face(mine, theirs)
        sign = -1.0 if side == 0 else 1.0
        edge[side, 0] = sign * mass
        edge[side, 1] = sign * second
        edge[side, 2] = sign * (first + GRAVITY * h * gz)

    ends = ((0, slice(0, 1)), (1, slice(rows - 1, rows)))

    def pack(k, block, carry):
        at = [(block * size + j, i, side, row) for j in range(size) for i in range(3) for side, row in ends]
        kept = [state[s, i, row] for s, i, side, row in at]
        for (s, i, side, row), x in zip(at, kept):
            rows_out[k, side, i, pl.ds(s, 1), :] = x
        return carry

    def close_rows(block, carry):
        at = [(block * size + j, i, side, row) for j in range(size) for i in range(3) for side, row in ends]
        closed = [tend[s, i, row] + edge[side, i, pl.ds(s, 1), :] for s, i, side, row in at]
        for (s, i, side, row), x in zip(at, closed):
            tend[s, i, row] = x
        return carry

    span_of = [(part * chunk // size, (part + 1) * chunk // size) for part in range(parts)]

    def send_rows(k, part):
        lax.fori_loop(*span_of[part], functools.partial(pack, k), 0)
        for copy in row_copies(k, part):
            copy.start()

    def send_tops(k):
        for copy in top_copies(k):
            copy.start()

    send_tops(0)
    for part in range(parts):
        send_rows(0, part)

    def step(k, carry):
        @pl.when(k == 0)
        def _():
            terrain_in.wait()
            slots(ground, 4)
            for copy in z_copies:
                copy.start()
            slots(prepare, 2)

        lax.fori_loop(0, listed // size, derive, 0)
        slots(balance, 2)

        @pl.when(k == 0)
        def _():
            for copy in z_copies:
                copy.wait_recv()
            for side in range(2):
                place_rows(side, z_in.at[side], ghost_z, [()])

        for part in range(parts):
            for copy in row_copies(k, part):
                copy.wait_recv()
        for side in range(2):
            place_rows(side, rows_in.at[k, side], ghost, [(0,), (1,), (2,)])
            rim(k, side)
        lax.fori_loop(0, listed // size, close_rows, 0)

        all_tops(k).wait_recv()
        top = jnp.maximum(jnp.max(top_in[k], axis=0), top_out[k])
        top = jnp.max(top, axis=1, keepdims=True)
        span = jnp.broadcast_to((COURANT / top) * 0.5, (rows, width))

        def update(i, top):
            block = pl.ds(i * size, size)
            h = state[block, 0] - span * tend[block, 0]
            root = lax.rsqrt(1.0 + span * tend[block, 3])
            damping = root * root
            p = (state[block, 1] - span * tend[block, 1]) * damping
            q = (state[block, 2] - span * tend[block, 2]) * damping
            return settle(i * size, size, h, p, q, top)

        top = jnp.zeros((rows, width), jnp.float32)
        for part in range(parts):
            top = lax.fori_loop(*span_of[part], update, top)
            pl.when(k + 1 < ITERS)(functools.partial(send_rows, k + 1, part))
        publish(k + 1, top)
        pl.when(k + 1 < ITERS)(functools.partial(send_tops, k + 1))
        return carry

    lax.fori_loop(0, ITERS, step, 0)

    spread = next(d for d in (4, 2, 1) if count_tiles % d == 0)

    def merge(i, carry):
        for j in range(spread):
            t = i * spread + j
            slot = owner[t]
            out[t] = jnp.where(slot >= 0, state[jnp.maximum(slot, 0)], wv[t])
        return carry

    lax.fori_loop(0, count_tiles // spread, merge, 0)

    for copy in z_copies:
        copy.wait_send()
    for k in range(ITERS):
        for part in range(parts):
            for copy in row_copies(k, part):
                copy.wait_send()
        all_tops(k).wait_send()


def body(n, water_state, terrain, work_list, edge_kind):
    count_tiles, _, rows, width = water_state.shape
    listed = work_list.shape[0]
    parts = 2 if listed % 16 == 0 else 1
    smem = pl.BlockSpec(memory_space=pltpu.SMEM)
    anywhere = pl.BlockSpec(memory_space=pl.ANY)
    f32 = jnp.float32

    def vmem(*shape, dtype=f32):
        return pltpu.VMEM(shape, dtype)

    dma = pltpu.SemaphoreType.DMA
    return pl.pallas_call(
        functools.partial(stepper, n, parts),
        out_shape=jax.ShapeDtypeStruct(water_state.shape, f32),
        in_specs=[smem, smem, anywhere, anywhere],
        out_specs=pl.BlockSpec(memory_space=pltpu.VMEM),
        scratch_shapes=[
            vmem(listed, 3, rows, width),
            vmem(count_tiles, 3, rows, width),
            vmem(count_tiles, 2, rows, width),
            vmem(listed, rows, width),
            vmem(listed, rows, width),
            vmem(listed, rows, width),
            vmem(listed, rows, width),
            vmem(listed, 6, rows, width),
            vmem(listed, 4, rows, width),
            vmem(ITERS, 2, 3, listed, width),
            vmem(ITERS, 2, 3, listed, width),
            vmem(2, listed, width),
            vmem(2, listed, width),
            vmem(2, 3, listed, width),
            vmem(2, listed, width),
            vmem(3, listed, width),
            vmem(2, 3, listed, width),
            vmem(2, listed, width, dtype=jnp.int32),
            vmem(ITERS + 1, 1, width // 2),
            vmem(ITERS, n - 1, 1, width // 2),
            pltpu.SMEM((8, listed), jnp.int32),
            pltpu.SMEM((count_tiles,), jnp.int32),
            dma((2,)),
            dma((ITERS,)),
            dma((ITERS,)),
            dma((ITERS, 2, parts)),
            dma((ITERS, 2, parts)),
            dma((2,)),
            dma((2,)),
        ],
        compiler_params=pltpu.CompilerParams(
            collective_id=0, has_side_effects=True, vmem_limit_bytes=48 * 1024 * 1024
        ),
    )(*[pltpu.with_memory_space_constraint(x, pltpu.HBM) for x in (work_list, edge_kind.T, water_state, terrain)])

def solution(mesh):
    placed = (
        P("groups", None, "tiles", None),
        P("groups", None, "tiles", None),
        P("groups"),
        P("groups", None),
    )
    return jax.shard_map(
        functools.partial(body, mesh.shape["tiles"]),
        mesh=mesh,
        in_specs=placed,
        out_specs=P("groups", None, "tiles", None),
        check_vma=False,
    )
```

```python
import functools

import jax
import jax.numpy as jnp
from jax import lax
from jax.experimental import pallas as pl
from jax.experimental.pallas import tpu as pltpu
from jax.sharding import PartitionSpec as P

TW = 16
ITERS = 4


GRAVITY = 9.81
DRY_DEPTH = 0.25
COURANT = 0.45


def roll_rows(x, shift):
    rows = x.shape[0]
    if rows % 8 == 0:
        return pltpu.roll(x, shift % rows, 0)
    cut = (rows - shift) % rows
    return jnp.concatenate([x[cut:], x[:cut]], axis=0)


def roll_lanes(x, shift):
    return pltpu.roll(x, shift % x.shape[1], 1)


def face(left, right):
    reach = jnp.maximum(left[1], right[1])
    mass = (left[0] + right[0]) - reach * (right[2] - left[2])
    first = (left[3] + right[3]) - reach * (right[0] - left[0])
    second = (left[4] + right[4]) - reach * (right[5] - left[5])
    return mass, first, second


def speeds(h, p, q):
    floored = jnp.maximum(h, DRY_DEPTH)
    root = lax.rsqrt(floored)
    inverse = root * root
    return p * inverse, q * inverse, (GRAVITY**0.5) * (floored * root)


def stepper(n, parts, work, kinds, water, terrain, out, state, wv, tv, zs, rough, slope_x, slope_y, derived,
            tend, rows_out, rows_in, z_out, z_in, ghost, ghost_z, landed, edge, edge_kinds, top_out, top_in,
            near, owner, local_sem, top_send, top_recv, row_send, row_recv, z_send, z_recv):
    count_tiles = water.shape[0]
    listed = state.shape[0]
    rows, width = state.shape[2], state.shape[3]
    half = width // 2
    me = lax.axis_index("tiles")
    at_first = me == 0
    at_final = me == n - 1

    chunk = listed // parts
    others = [{"tiles": jnp.where(me + d < n, me + d, me + d - n)} for d in range(1, n)]
    down, up = others[0], others[-1]
    barrier = pltpu.get_barrier_semaphore()
    for other in others:
        pl.semaphore_signal(barrier, inc=1, device_id=other, device_id_type=pl.DeviceIdType.MESH)
    water_in = pltpu.make_async_copy(water, wv, local_sem.at[0])
    terrain_in = pltpu.make_async_copy(terrain, tv, local_sem.at[1])
    water_in.start()
    terrain_in.start()

    entries = [work[j] for j in range(listed)]

    def locate(s, carry):
        tile = work[s]
        chosen = jnp.minimum(tile, count_tiles - 1)
        active = tile < count_tiles
        found = [jnp.int32(0)] * 4
        sides = (chosen - TW, chosen + TW, chosen - 1, chosen + 1)
        for j in range(listed):
            found = [jnp.where(entries[j] == side, j, f) for side, f in zip(sides, found)]
        for e in range(4):
            near[e, s] = found[e]
            kind = jnp.where(active, kinds[e, chosen], 0)
            near[4 + e, s] = kind
            if e < 2:
                outer = jnp.where(at_first if e == 0 else at_final, kind, 1)
                edge_kinds[e, pl.ds(s, 1), :] = jnp.full((1, width), outer, jnp.int32)
        return carry

    lax.fori_loop(0, listed, locate, 0)

    def slots(one, unroll, carry=0):
        unroll = unroll if listed % unroll == 0 else 1

        def several(i, carry):
            for j in range(unroll):
                carry = one(i * unroll + j, carry)
            return carry

        return lax.fori_loop(0, listed // unroll, several, carry)

    row_at = lax.broadcasted_iota(jnp.int32, (rows, width), 0)
    lane_at = lax.broadcasted_iota(jnp.int32, (rows, half), 1)
    inner = row_at < rows - 1

    def settle(s, size, h, p, q, top):
        u, v, c = speeds(h, p, q)
        block = pl.ds(s, size)
        for i, x in enumerate((h, p, q)):
            state[block, i] = x
        fastest = jnp.maximum(jnp.abs(u), jnp.abs(v)) + c
        for j in range(size):
            top = jnp.maximum(top, jnp.where(work[s + j] < count_tiles, fastest[j], 0.0))
        return top

    def publish(k, top):
        part = jnp.max(top, axis=0, keepdims=True)
        top_out[k] = jnp.maximum(part[:, :half], part[:, half:])

    water_in.wait()

    def gather(s, top):
        chosen = jnp.minimum(work[s], count_tiles - 1)
        return settle(s, 1, *[wv[pl.ds(chosen, 1), i] for i in range(3)], top)

    publish(0, slots(gather, 4, jnp.zeros((rows, width), jnp.float32)))
    pl.semaphore_wait(barrier, n - 1)

    def remote(src, dst, send, recv, to):
        return pltpu.make_async_remote_copy(
            src_ref=src, dst_ref=dst, send_sem=send, recv_sem=recv, device_id=to,
            device_id_type=pl.DeviceIdType.MESH,
        )

    def top_copies(k):
        return [
            remote(top_out.at[k], top_in.at[k, i], top_send.at[k], top_recv.at[k], other)
            for i, other in enumerate(others)
        ]

    def all_tops(k):
        return remote(top_in.at[k], top_in.at[k], top_send.at[k], top_recv.at[k], down)

    def row_copies(k, part):
        block = pl.ds(part * chunk, chunk)
        return [
            remote(rows_out.at[k, 0, :, block], rows_in.at[k, 1, :, block],
                   row_send.at[k, 0, part], row_recv.at[k, 1, part], up),
            remote(rows_out.at[k, 1, :, block], rows_in.at[k, 0, :, block],
                   row_send.at[k, 1, part], row_recv.at[k, 0, part], down),
        ]

    z_copies = [
        remote(z_out.at[0], z_in.at[1], z_send.at[0], z_recv.at[1], up),
        remote(z_out.at[1], z_in.at[0], z_send.at[1], z_recv.at[0], down),
    ]

    def ground(s, carry):
        z = tv[jnp.minimum(work[s], count_tiles - 1), 0]
        zs[s] = z
        z_out[0, pl.ds(s, 1), :] = z[:1]
        z_out[1, pl.ds(s, 1), :] = z[rows - 1 :]
        return carry

    def prepare(s, carry):
        chosen = jnp.minimum(work[s], count_tiles - 1)
        z = zs[s]
        manning = tv[chosen, 1]
        rough[s] = (2.0 * GRAVITY) * manning * manning
        west_z = zs[near[2, s]][:, half:]
        east_z = zs[near[3, s]][:, :half]
        west_open = near[6, s] == 1
        east_open = near[7, s] == 1
        z_low, z_high = z[:, :half], z[:, half:]
        to_east = roll_lanes(z, -1)
        to_west = roll_lanes(z, 1)
        last = jnp.where(east_open, roll_lanes(east_z, -1), z_high)
        first = jnp.where(west_open, roll_lanes(west_z, 1), z_low)
        east = jnp.concatenate([to_east[:, :half], jnp.where(lane_at == half - 1, last, to_east[:, half:])], axis=1)
        west = jnp.concatenate([jnp.where(lane_at == 0, first, to_west[:, :half]), to_west[:, half:]], axis=1)
        slope_x[s] = GRAVITY * (east - west)
        south = jnp.where(inner, roll_rows(z, -1), 0.0)
        north = jnp.where(row_at == 0, 0.0, roll_rows(z, 1))
        slope_y[s] = GRAVITY * (south - north)
        share = -(-count_tiles // listed)
        for j in range(share):
            tile = jnp.minimum(s * share + j, count_tiles - 1)
            slot = jnp.int32(-1)
            for i in range(listed):
                slot = jnp.where(entries[i] == tile, i, slot)
            owner[tile] = slot
        return carry

    size = next(d for d in (4, 2, 1) if chunk % d == 0)

    def derive(i, carry):
        block = pl.ds(i * size, size)
        h, p, q = state[block, 0], state[block, 1], state[block, 2]
        u, v, c = speeds(h, p, q)
        pressure = (0.5 * GRAVITY) * h * h
        derived[block, 0] = jnp.abs(u) + c
        derived[block, 1] = h + zs[block]
        derived[block, 2] = p * u + pressure
        derived[block, 3] = q * u
        derived[block, 4] = jnp.abs(v) + c
        derived[block, 5] = q * v + pressure
        floored = jnp.maximum(h, DRY_DEPTH)
        resist = jnp.exp(jnp.log(floored) * (-7.0 / 3.0))
        tend[block, 3] = rough[block] * jnp.sqrt(p * p + q * q) * resist
        return carry

    def along(s, lanes):
        return (state[s, 1, :, lanes], derived[s, 0, :, lanes], derived[s, 1, :, lanes],
                derived[s, 2, :, lanes], derived[s, 3, :, lanes], state[s, 2, :, lanes])

    low, high, whole = pl.ds(0, half), pl.ds(half, half), pl.ds(0, width)

    def balance(s, carry):
        own = along(s, whole)
        own_low = [x[:, :half] for x in own]
        own_high = [x[:, half:] for x in own]
        from_west = along(near[2, s], high)
        from_east = along(near[3, s], low)
        west_kind, east_kind = near[6, s], near[7, s]

        beyond = [
            roll_lanes(jnp.concatenate([jnp.where(lane_at == 0, g, a), b], axis=1), -1)
            for g, a, b in zip(from_east, own_low, own_high)
        ]
        flux = face(own, beyond)
        closed = 2.0 * own_high[1] * own_high[0]
        shut = (
            jnp.where(east_kind == 2, 2.0 * own_high[0], 0.0),
            2.0 * own_high[3] + jnp.where(east_kind == 0, closed, 0.0),
            jnp.where(east_kind == 2, 2.0 * own_high[4], 0.0),
        )
        rim = (lane_at == half - 1) & (east_kind != 1)
        flux = [
            jnp.concatenate([f[:, :half], jnp.where(rim, g, f[:, half:])], axis=1) for f, g in zip(flux, shut)
        ]
        entry = face([roll_lanes(x, 1) for x in from_west], own_low)
        closed = 2.0 * own_low[1] * own_low[0]
        shut = (
            jnp.where(west_kind == 2, 2.0 * own_low[0], 0.0),
            2.0 * own_low[3] - jnp.where(west_kind == 0, closed, 0.0),
            jnp.where(west_kind == 2, 2.0 * own_low[4], 0.0),
        )
        entry = [jnp.where(west_kind == 1, f, g) for f, g in zip(entry, shut)]
        change = []
        for f, g in zip(flux, entry):
            back = roll_lanes(f, 1)
            back = jnp.concatenate([jnp.where(lane_at == 0, g, back[:, :half]), back[:, half:]], axis=1)
            change.append(f - back)

        column = (own[5], derived[s, 4], own[2], derived[s, 5], own[4], own[0])
        flux = face(column, [roll_rows(x, -1) for x in column])
        flux = [jnp.where(inner, f, 0.0) for f in flux]
        across = [f - roll_rows(f, 1) for f in flux]
        h = state[s, 0]
        tend[s, 0] = change[0] + across[0]
        tend[s, 1] = change[1] + across[2] + h * slope_x[s]
        tend[s, 2] = change[2] + across[1] + h * slope_y[s]
        return carry

    def place_rows(side, source, target, channels):
        at_rim = at_first if side == 0 else at_final

        @pl.when(at_rim)
        def _():
            for i, index in enumerate(channels):
                landed[i] = source[index + (slice(None), slice(None))]

            def one(s, carry):
                nearby = near[side, s]
                for i, index in enumerate(channels):
                    target[(side,) + index + (pl.ds(s, 1), slice(None))] = landed[i, pl.ds(nearby, 1), :]
                return carry

            slots(one, 4)

        @pl.when(jnp.logical_not(at_rim))
        def _():
            target[side] = source[...]

    def rim_cells(h, p, q, z):
        u, v, c = speeds(h, p, q)
        return (q, jnp.abs(v) + c, h + z, q * v + (0.5 * GRAVITY) * h * h, q * u, p)

    def rim(k, side):
        open_edge = edge_kinds[side] == 1
        wall = edge_kinds[side] == 0
        h, p, q, z = rows_out[k, side, 0], rows_out[k, side, 1], rows_out[k, side, 2], z_out[side]
        gh = jnp.where(open_edge, ghost[side, 0], h)
        gp = jnp.where(open_edge, ghost[side, 1], p)
        gq = jnp.where(open_edge, ghost[side, 2], jnp.where(wall, -q, q))
        gz = jnp.where(open_edge, ghost_z[side], z)
        mine, theirs = rim_cells(h, p, q, z), rim_cells(gh, gp, gq, gz)
        mass, first, second = face(theirs, mine) if side == 0 else face(mine, theirs)
        sign = -1.0 if side == 0 else 1.0
        edge[side, 0] = sign * mass
        edge[side, 1] = sign * second
        edge[side, 2] = sign * (first + GRAVITY * h * gz)

    ends = ((0, slice(0, 1)), (1, slice(rows - 1, rows)))

    def pack(k, block, carry):
        at = [(block * size + j, i, side, row) for j in range(size) for i in range(3) for side, row in ends]
        kept = [state[s, i, row] for s, i, side, row in at]
        for (s, i, side, row), x in zip(at, kept):
            rows_out[k, side, i, pl.ds(s, 1), :] = x
        return carry

    def close_rows(block, carry):
        at = [(block * size + j, i, side, row) for j in range(size) for i in range(3) for side, row in ends]
        closed = [tend[s, i, row] + edge[side, i, pl.ds(s, 1), :] for s, i, side, row in at]
        for (s, i, side, row), x in zip(at, closed):
            tend[s, i, row] = x
        return carry

    span_of = [(part * chunk // size, (part + 1) * chunk // size) for part in range(parts)]

    def send_rows(k, part):
        lax.fori_loop(*span_of[part], functools.partial(pack, k), 0)
        for copy in row_copies(k, part):
            copy.start()

    def send_tops(k):
        for copy in top_copies(k):
            copy.start()

    send_tops(0)
    for part in range(parts):
        send_rows(0, part)

    def step(k, carry):
        @pl.when(k == 0)
        def _():
            terrain_in.wait()
            slots(ground, 4)
            for copy in z_copies:
                copy.start()
            slots(prepare, 2)

        lax.fori_loop(0, listed // size, derive, 0)
        slots(balance, 4)

        @pl.when(k == 0)
        def _():
            for copy in z_copies:
                copy.wait_recv()
            for side in range(2):
                place_rows(side, z_in.at[side], ghost_z, [()])

        for part in range(parts):
            for copy in row_copies(k, part):
                copy.wait_recv()
        for side in range(2):
            place_rows(side, rows_in.at[k, side], ghost, [(0,), (1,), (2,)])
            rim(k, side)
        lax.fori_loop(0, listed // size, close_rows, 0)

        all_tops(k).wait_recv()
        top = jnp.maximum(jnp.max(top_in[k], axis=0), top_out[k])
        top = jnp.max(top, axis=1, keepdims=True)
        span = jnp.broadcast_to((COURANT / top) * 0.5, (rows, width))

        def update(i, top):
            block = pl.ds(i * size, size)
            h = state[block, 0] - span * tend[block, 0]
            root = lax.rsqrt(1.0 + span * tend[block, 3])
            damping = root * root
            p = (state[block, 1] - span * tend[block, 1]) * damping
            q = (state[block, 2] - span * tend[block, 2]) * damping
            return settle(i * size, size, h, p, q, top)

        top = jnp.zeros((rows, width), jnp.float32)
        for part in range(parts):
            top = lax.fori_loop(*span_of[part], update, top)
            pl.when(k + 1 < ITERS)(functools.partial(send_rows, k + 1, part))
        publish(k + 1, top)
        pl.when(k + 1 < ITERS)(functools.partial(send_tops, k + 1))
        return carry

    lax.fori_loop(0, ITERS, step, 0)

    spread = next(d for d in (4, 2, 1) if count_tiles % d == 0)

    def merge(i, carry):
        for j in range(spread):
            t = i * spread + j
            slot = owner[t]
            out[t] = jnp.where(slot >= 0, state[jnp.maximum(slot, 0)], wv[t])
        return carry

    lax.fori_loop(0, count_tiles // spread, merge, 0)

    for copy in z_copies:
        copy.wait_send()
    for k in range(ITERS):
        for part in range(parts):
            for copy in row_copies(k, part):
                copy.wait_send()
        all_tops(k).wait_send()


def body(n, water_state, terrain, work_list, edge_kind):
    count_tiles, _, rows, width = water_state.shape
    listed = work_list.shape[0]
    parts = 2 if listed % 16 == 0 else 1
    smem = pl.BlockSpec(memory_space=pltpu.SMEM)
    anywhere = pl.BlockSpec(memory_space=pl.ANY)
    f32 = jnp.float32

    def vmem(*shape, dtype=f32):
        return pltpu.VMEM(shape, dtype)

    dma = pltpu.SemaphoreType.DMA
    return pl.pallas_call(
        functools.partial(stepper, n, parts),
        out_shape=jax.ShapeDtypeStruct(water_state.shape, f32),
        in_specs=[smem, smem, anywhere, anywhere],
        out_specs=pl.BlockSpec(memory_space=pltpu.VMEM),
        scratch_shapes=[
            vmem(listed, 3, rows, width),
            vmem(count_tiles, 3, rows, width),
            vmem(count_tiles, 2, rows, width),
            vmem(listed, rows, width),
            vmem(listed, rows, width),
            vmem(listed, rows, width),
            vmem(listed, rows, width),
            vmem(listed, 6, rows, width),
            vmem(listed, 4, rows, width),
            vmem(ITERS, 2, 3, listed, width),
            vmem(ITERS, 2, 3, listed, width),
            vmem(2, listed, width),
            vmem(2, listed, width),
            vmem(2, 3, listed, width),
            vmem(2, listed, width),
            vmem(3, listed, width),
            vmem(2, 3, listed, width),
            vmem(2, listed, width, dtype=jnp.int32),
            vmem(ITERS + 1, 1, width // 2),
            vmem(ITERS, n - 1, 1, width // 2),
            pltpu.SMEM((8, listed), jnp.int32),
            pltpu.SMEM((count_tiles,), jnp.int32),
            dma((2,)),
            dma((ITERS,)),
            dma((ITERS,)),
            dma((ITERS, 2, parts)),
            dma((ITERS, 2, parts)),
            dma((2,)),
            dma((2,)),
        ],
        compiler_params=pltpu.CompilerParams(
            collective_id=0, has_side_effects=True, vmem_limit_bytes=48 * 1024 * 1024
        ),
    )(*[pltpu.with_memory_space_constraint(x, pltpu.HBM) for x in (work_list, edge_kind.T, water_state, terrain)])

def solution(mesh):
    placed = (
        P("groups", None, "tiles", None),
        P("groups", None, "tiles", None),
        P("groups"),
        P("groups", None),
    )
    return jax.shard_map(
        functools.partial(body, mesh.shape["tiles"]),
        mesh=mesh,
        in_specs=placed,
        out_specs=P("groups", None, "tiles", None),
        check_vma=False,
    )
```
